128 devices in a mesh: space: 32 (over z, y, core), slab: 4 (over x).
Axes of the slice: x: 4, y: 4, z: 4, core: 2. Of those that a mesh axis runs over, the one named last changes fastest.
Arguments:
- features: float32 [512, 8, 8, 512], P(('space', 'slab')), may hold values from -6 to 6
- live: int32 [128], P(('space', 'slab')), may hold values from 1 to 4, as said below
- rim_slots: int32 [128, 2], P(('space', 'slab')), may hold values from 0 to 3, as said below
- neighbours: int32 [512, 26], P(('space', 'slab')), may hold values from 0 to 12, as said below
- weights: float32 [4, 27, 4096], replicated, may hold values from -0.15625 to 0.15625
- biases: float32 [4, 64], replicated, may hold values from -3 to 3
Outputs:
- output: float32 [512, 8, 8, 512], P(('space', 'slab'))
The draws below stay inside these ranges and needn't reach their ends.
Inputs may be any that keep to these rules, and one draw needn't show every extreme that they name: `live`: devices whose space indices differ by 32 / 2 (same slab index) hold at most 6 occupied bricks together; in every draw some pair holds exactly that and some device holds 4. `rim_slots`: every entry is below its device's live count. `neighbours`: entries below 4 are below the device's live count.
All inputs are finite; a program needn't handle non-finite values.
Results may differ from the reference program's by a relative error of at most 0.0003.
Values sent between devices are 32-bit elements; how exact they have to be, the bound alone decides.
No kernel may reach another device: no remote copies, remote signals or barrier semaphores. Data moves between devices by JAX's collectives and lax.ppermute only.
A program may use at most 128 MiB of HBM per device.

```python
import jax
import jax.numpy as jnp
from jax import lax

CH = 64
CONVS = 4
B_DEV = 4
RIM = 2
LEND = 3
BRICKS = 512
N_SPACE = 32
N_SLAB = 4


def live_counts(key):
    base = jax.random.fold_in(key, 11)
    kone, ktwo, kthree, kfour = jax.random.split(base, 4)
    half = N_SPACE // 2
    pairs = half * N_SLAB
    heavy = jax.random.randint(kone, (pairs,), LEND, B_DEV + 1)
    spread = jax.random.randint(ktwo, (pairs,), 0, 1 << 20)
    light = 1 + spread % (2 * LEND - heavy)
    forced = jax.random.randint(kthree, (), 0, pairs)
    index = jnp.arange(pairs)
    heavy = jnp.where(index == forced, B_DEV, heavy)
    light = jnp.where(index == forced, 2 * LEND - B_DEV, light)
    flip = jax.random.randint(kfour, (pairs,), 0, 2)
    first = jnp.where(flip == 1, heavy, light).reshape(half, N_SLAB)
    second = jnp.where(flip == 1, light, heavy).reshape(half, N_SLAB)
    return jnp.concatenate([first, second], 0).reshape(-1).astype(jnp.int32)


def draw_live(key, part):
    return live_counts(key)


def draw_rim_slots(key, part):
    counts = live_counts(key)
    spread = jax.random.randint(jax.random.fold_in(key, 23), (N_SPACE * N_SLAB, RIM), 0, 1 << 20)
    return (spread % counts[:, None]).astype(jnp.int32)


def draw_neighbours(key, part):
    counts = live_counts(key)
    rows = N_SPACE * N_SLAB * B_DEV
    owner_live = jnp.repeat(counts, B_DEV)[:, None]
    kone, ktwo = jax.random.split(jax.random.fold_in(key, 37))
    kind = jax.random.randint(kone, (rows, 26), 0, 5)
    spread = jax.random.randint(ktwo, (rows, 26), 0, 1 << 20)
    own = spread % owner_live
    rim = B_DEV + spread % (4 * RIM)
    empty = jnp.full((rows, 26), B_DEV + 4 * RIM, jnp.int32)
    return jnp.where(kind < 2, own, jnp.where(kind < 4, rim, empty)).astype(jnp.int32)


def block_scale(stream_key, dims, cuts, smallest, top_value):
    level = 1.0
    for axis_at, blocks in cuts:
        heights = jax.random.uniform(jax.random.fold_in(jax.random.fold_in(stream_key, 6), axis_at), (blocks,), jnp.float32, smallest / len(cuts), top_value / len(cuts))
        level = level * jnp.repeat(jnp.exp(heights), dims[axis_at] // blocks).reshape((-1,) + (1,) * (len(dims) - 1 - axis_at))
    return level


def noise(stream_key, shape, deviation, most, cuts=(), held_as=jnp.bfloat16):
    factor_of = block_scale(stream_key, shape, cuts, -0.22, 0.18) if cuts else 1.0
    array = jax.random.normal(stream_key, shape, jnp.float32) * deviation * factor_of
    return jnp.minimum(jnp.maximum(array, -most), most).astype(held_as)


def setup_inputs(seed: int = 0) -> dict:
    arg_keys = jax.random.split(jax.random.key(seed), 7)
    return {
        "features": noise(arg_keys[0], (BRICKS, 8, 8, 8 * CH), 1.0, 6.0, ((0, 128),), jnp.float32),
        "live": draw_live(jax.random.fold_in(arg_keys[6], 71), 0),
        "rim_slots": draw_rim_slots(jax.random.fold_in(arg_keys[6], 71), 0),
        "neighbours": draw_neighbours(jax.random.fold_in(arg_keys[6], 71), 0),
        "weights": noise(arg_keys[4], (CONVS, 27, CH * CH), (27 * CH) ** -0.5, 0.15625, (), jnp.float32),
        "biases": noise(arg_keys[5], (CONVS, CH), 0.5, 3.0, (), jnp.float32),
    }


def direction_list():
    result = []
    for ddx in (-1, 0, 1):
        for ddy in (-1, 0, 1):
            for ddz in (-1, 0, 1):
                if (ddx, ddy, ddz) != (0, 0, 0):
                    result.append((ddx, ddy, ddz))
    return result


def source_index(step):
    if step == -1:
        return 7
    if step == 1:
        return 0
    return slice(0, 8)


def extent(step):
    return 8 if step == 0 else 1


def brick_piece(table, direction):
    ddx, ddy, ddz = direction
    channels = table.shape[-1] // 8
    cube = table.reshape(table.shape[0], 8, 8, 8, channels)
    return cube[:, source_index(ddx), source_index(ddy), source_index(ddz)]


def assemble(center, table, nbr, getter):
    count = center.shape[0]
    channels = center.shape[-1] // 8
    blocks = {(0, 0, 0): center.reshape(count, 8, 8, 8, channels)}
    for jdir, direction in enumerate(direction_list()):
        piece = getter(table, direction)[nbr[:, jdir]]
        blocks[direction] = piece.reshape(count, extent(direction[0]), extent(direction[1]), extent(direction[2]), channels)
    slabs = []
    for ddx in (-1, 0, 1):
        rows = []
        for ddy in (-1, 0, 1):
            rows.append(jnp.concatenate([blocks[(ddx, ddy, ddz)] for ddz in (-1, 0, 1)], 3))
        slabs.append(jnp.concatenate(rows, 2))
    return jnp.concatenate(slabs, 1)


def convolve(padded, kernel):
    count = padded.shape[0]
    channels = padded.shape[-1]
    taps = kernel.reshape(27, channels, channels)
    stacked = jnp.concatenate([padded[:, :, boff:boff + 8, coff:coff + 8, :] for boff in range(3) for coff in range(3)], -1)
    total = jnp.zeros((count * 512, channels), jnp.float32)
    for aoff in range(3):
        columns = stacked[:, aoff:aoff + 8].reshape(count * 512, 9 * channels)
        block = taps[aoff * 9:aoff * 9 + 9].reshape(9 * channels, channels)
        total = total + jnp.dot(columns, block, preferred_element_type=jnp.float32, precision=lax.Precision.HIGHEST)
    return total.reshape(count, 8, 8, 8 * channels)


def reference(features, live, rim_slots, neighbours, weights, biases):
    devices = N_SPACE * N_SLAB
    width = 8 * CH
    field = features.reshape(devices, B_DEV, 8, 8, width)
    mask = (jnp.arange(B_DEV, dtype=jnp.int32)[None, :] < live[:, None]).astype(jnp.float32)[:, :, None, None, None]
    nbr = neighbours.reshape(devices, B_DEV, 26)

    def layer(field, kidx):
        rims = jax.vmap(lambda rows, slots: rows[slots])(field, rim_slots)
        grid = rims.reshape(N_SPACE, N_SLAB, RIM, 8, 8, width)
        zero_row = jnp.zeros((1, N_SLAB, RIM, 8, 8, width), jnp.float32)
        zero_col = jnp.zeros((N_SPACE, 1, RIM, 8, 8, width), jnp.float32)
        low_space = jnp.concatenate([zero_row, grid[:-1]], 0)
        high_space = jnp.concatenate([grid[1:], zero_row], 0)
        low_slab = jnp.concatenate([zero_col, grid[:, :-1]], 1)
        high_slab = jnp.concatenate([grid[:, 1:], zero_col], 1)
        beside_all = jnp.concatenate([low_space, high_space, low_slab, high_slab], 2).reshape(devices, 4 * RIM, 8, 8, width)
        table = jnp.concatenate([field, beside_all, jnp.zeros((devices, 1, 8, 8, width), jnp.float32)], 1)

        def single(items):
            tab, cen, nb = items
            return convolve(assemble(cen, tab, nb, brick_piece), weights[kidx])

        return lax.map(single, (table, field, nbr))

    field = field * mask
    for blk in range(CONVS // 2):
        first = 2 * blk
        hidden = jax.nn.relu(layer(field, first) + jnp.tile(biases[first], 8)) * mask
        field = jax.nn.relu(field + layer(hidden, first + 1) + jnp.tile(biases[first + 1], 8)) * mask
    return field.reshape(devices * B_DEV, 8, 8, width)
```

```python
import functools

import jax
import jax.numpy as jnp
from jax import lax
from jax.experimental import pallas as pl
from jax.experimental.pallas import tpu as pltpu
from jax.sharding import PartitionSpec as P

BRICK = 4
FACE = 192
MIB = 1 << 20
VM = pl.BlockSpec(memory_space=pltpu.VMEM)
SM = pl.BlockSpec(memory_space=pltpu.SMEM)
F32, BF16 = jnp.float32, jnp.bfloat16


def direction(dx, dy, dz):
    at = (dx + 1) * 9 + (dy + 1) * 3 + dz + 1
    return at - (at > 13)


def lower_half(shape):
    return lax.broadcasted_iota(jnp.int32, shape, len(shape) - 1) < 64


def write_faces(field, faces):
    low = lower_half((8, 128))
    for b in range(BRICK):
        for s in range(2):
            for i in range(8):
                col = (7 * s * 8 + i) * 16 + 4 * b
                faces[b, 32 * s + 4 * i : 32 * s + 4 * i + 4, :] = field[col : col + 4, :]
                col = (i * 8 + 7 * s) * 16 + 4 * b
                at = 64 + 32 * s + 4 * i
                faces[b, at : at + 4, :] = field[col : col + 4, :]
        for x in range(8):
            first = field[pl.ds(x * 128 + 4 * b, 8, stride=16), :]
            last = field[pl.ds(x * 128 + 4 * b + 3, 8, stride=16), :]
            faces[b, 128 + 8 * x : 136 + 8 * x, :] = jnp.where(low, first, last)


def offer(slots, faces, send):
    for e in range(2):
        send[e] = faces[slots[0, e]]


def entry_kernel(live, slots, feat, field, faces, send):
    count = live[0]
    for b in range(BRICK):
        keep = jnp.where(b < count, 1.0, 0.0).astype(F32)
        for x in range(8):
            for q in range(4):
                tile = feat[b, x, :, 128 * q : 128 * q + 128] * keep
                field[pl.ds(x * 128 + 4 * b + q, 8, stride=16), :] = tile
    write_faces(field, faces)
    offer(slots, faces, send)


def taps_kernel(weights, taps, even, odd, wide):
    low = lower_half((32, 128))
    zero = jnp.zeros((32, 128), F32)
    for k in range(weights.shape[0]):
        for g in range(4):
            n = 8 if g < 3 else 3
            for i in range(32):
                tile = weights[k, 8 * g : 8 * g + n, 128 * i : 128 * i + 128]
                even[pl.ds(8 * g * 32 + i, n, stride=32), :] = tile
                odd[pl.ds(8 * g * 32 + i, n, stride=32), :] = pltpu.roll(tile, 64, 1)
        for t in range(9):
            def rows(ref, d):
                if d < 0 or d > 2:
                    return zero
                return ref[(3 * t + d) * 32 : (3 * t + d) * 32 + 32, :]

            for w, base in ((0, 192), (1, 0), (2, 64), (3, 128)):
                wide[pl.ds(base, 32, stride=2), :] = jnp.where(low, rows(even, w), rows(odd, w - 1))
                wide[pl.ds(base + 1, 32, stride=2), :] = jnp.where(low, rows(odd, w), rows(even, w - 1))
            full = wide[...]
            high = full.astype(BF16)
            taps[k, t, :, 0:128] = high
            taps[k, t, :, 128:256] = (full - high.astype(F32)).astype(BF16)


def fill_table(faces, arrived, table):
    table[0:4] = faces[...]
    for k, ref in enumerate(arrived):
        table[4 + 2 * k : 6 + 2 * k] = ref[...]
    table[12] = jnp.zeros((FACE, 128), F32)


def fill_margins(nbr, field, table, one, two):
    for x in range(8):
        one[(x + 1) * 160 + 16 : (x + 1) * 160 + 144, :] = field[x * 128 : x * 128 + 128, :]
    for b in range(BRICK):
        def cell(xp, yp):
            return (xp * 10 + yp) * 16 + 4 * b

        for d in (-1, 1):
            s, p = (1, 0) if d < 0 else (0, 9)
            t = nbr[b, direction(d, 0, 0)]
            for i in range(8):
                at = cell(p, i + 1)
                one[at : at + 4, :] = table[t, 32 * s + 4 * i : 32 * s + 4 * i + 4, :]
            t = nbr[b, direction(0, d, 0)]
            for i in range(8):
                at = cell(i + 1, p)
                one[at : at + 4, :] = table[t, 64 + 32 * s + 4 * i : 64 + 32 * s + 4 * i + 4, :]
            for e in (-1, 1):
                y, py = (7, 0) if e < 0 else (0, 9)
                t = nbr[b, direction(d, e, 0)]
                at = cell(p, py)
                one[at : at + 4, :] = table[t, 32 * s + 4 * y : 32 * s + 4 * y + 4, :]
    low3 = lower_half((20, 8, 128))
    for c in range(10):
        rows = one[c * 160 : c * 160 + 160, :].reshape(20, 8, 128)
        both = jnp.where(low3, pltpu.roll(rows, 7, 1), pltpu.roll(rows, 1, 1))
        two[c * 160 : c * 160 + 160, :] = both.reshape(160, 128)
    low = lower_half((8, 128))
    low1 = lower_half((1, 128))
    for b in range(BRICK):
        for dz in (-1, 1):
            def merge(start, stride, new):
                at = pl.ds(start, 8, stride=stride)
                old = two[at, :]
                two[at, :] = jnp.where(low, new, old) if dz > 0 else jnp.where(low, old, new)

            row = 4 * b + (3 if dz > 0 else 0)
            t = nbr[b, direction(0, 0, dz)]
            for x in range(8):
                merge(((x + 1) * 10 + 1) * 16 + row, 16, table[t, 128 + 8 * x : 136 + 8 * x, :])
            for d in (-1, 1):
                x, p = (7, 0) if d < 0 else (0, 9)
                t = nbr[b, direction(d, 0, dz)]
                merge((p * 10 + 1) * 16 + row, 16, table[t, 128 + 8 * x : 136 + 8 * x, :])
                t = nbr[b, direction(0, d, dz)]
                merge((10 + p) * 16 + row, 160, table[t, pl.ds(128 + x, 8, stride=8), :])
                for e in (-1, 1):
                    y, py = (7, 0) if e < 0 else (0, 9)
                    t = nbr[b, direction(d, e, dz)]
                    at = (p * 10 + py) * 16 + row
                    new = table[t, 128 + 8 * x + y : 129 + 8 * x + y, :]
                    old = two[at : at + 1, :]
                    two[at : at + 1, :] = jnp.where(low1, new, old) if dz > 0 else jnp.where(low1, old, new)


def split(one, two, high, rest):
    for c in range(10):
        for half, ref in enumerate((one, two)):
            full = ref[c * 160 : c * 160 + 160, :]
            top = full.astype(BF16)
            high[c, :, 128 * half : 128 * half + 128] = top
            rest[c, :, 128 * half : 128 * half + 128] = (full - top.astype(F32)).astype(BF16)


def convolve(high, rest, taps):
    wide = None
    narrow = None
    for dx in range(3):
        for dy in range(3):
            kernel = taps[3 * dx + dy]
            rows = high[dx : dx + 8, dy * 16 : dy * 16 + 128, :].reshape(1024, 256)
            part = jnp.dot(rows, kernel, preferred_element_type=F32)
            wide = part if wide is None else wide + part
            rows = rest[dx : dx + 8, dy * 16 : dy * 16 + 128, :].reshape(1024, 256)
            part = jnp.dot(rows, kernel[:, 0:128], preferred_element_type=F32)
            narrow = part if narrow is None else narrow + part
    return wide[:, 0:128] + (wide[:, 128:256] + narrow)


def layer_kernel(residual, last, index, live, slots, nbr, *refs):
    refs = list(refs)
    field, faces = refs[:2]
    arrived = refs[2:6]
    taps, biases = refs[6:8]
    refs = refs[8:]
    skip = refs.pop(0) if residual else None
    if last:
        (out,) = refs[:1]
        refs = refs[1:]
        table, one, two, high, rest, new = refs
    else:
        new, new_faces, send = refs[:3]
        table, one, two, high, rest = refs[3:]
    fill_table(faces, arrived, table)
    fill_margins(nbr, field, table, one, two)
    split(one, two, high, rest)
    total = convolve(high, rest, taps.at[index])
    bias = biases[index : index + 1, :]
    total = total + jnp.concatenate([bias, bias], 1)
    if residual:
        total = total + skip[...]
    brick = lax.broadcasted_iota(jnp.int32, (1024, 128), 0) % 16 // 4
    new[...] = jnp.where(brick < live[0], jnp.maximum(total, 0.0), 0.0)
    if last:
        for b in range(BRICK):
            for x in range(8):
                for q in range(4):
                    out[b, x, :, 128 * q : 128 * q + 128] = new[pl.ds(x * 128 + 4 * b + q, 8, stride=16), :]
    else:
        write_faces(new, new_faces)
        offer(slots, new_faces, send)


FIELD = jax.ShapeDtypeStruct((1024, 128), F32)
FACES = jax.ShapeDtypeStruct((BRICK, FACE, 128), F32)
SEND = jax.ShapeDtypeStruct((2, FACE, 128), F32)


def swaps(size, first):
    pairs = [(i, i + 1) for i in range(first, size - 1, 2)]
    return pairs + [(b, a) for a, b in pairs]


def exchange(send):
    got = []
    for axis in ("space", "slab"):
        size = lax.axis_size(axis)
        near = lax.ppermute(send, axis, swaps(size, 0))
        far = lax.ppermute(send, axis, swaps(size, 1))
        odd = lax.axis_index(axis) % 2 == 1
        got.append((near, far, odd))
    out = []
    for near, far, odd in got:
        out += [jnp.where(odd, near, far), jnp.where(odd, far, near)]
    return out


def shards(features, live, rim_slots, neighbours, weights, biases):
    params = pltpu.CompilerParams(vmem_limit_bytes=24 * MIB)
    field, faces, send = pl.pallas_call(
        entry_kernel,
        out_shape=(FIELD, FACES, SEND),
        in_specs=[SM, SM, VM],
        out_specs=(VM, VM, VM),
        compiler_params=params,
        name="entry",
    )(live, rim_slots, features)
    convs = weights.shape[0]
    taps = pl.pallas_call(
        taps_kernel,
        out_shape=jax.ShapeDtypeStruct((convs, 9, 256, 256), BF16),
        in_specs=[VM],
        out_specs=VM,
        scratch_shapes=[pltpu.VMEM((896, 128), F32), pltpu.VMEM((896, 128), F32), pltpu.VMEM((256, 128), F32)],
        compiler_params=params,
        name="taps",
    )(weights)

    def layer(index, field, faces, send, skip, last):
        arrived = exchange(send)
        args = [live, rim_slots, neighbours, field, faces, *arrived, taps, biases]
        if skip is not None:
            args.append(skip)
        out_shape = (jax.ShapeDtypeStruct(features.shape, F32),) if last else (FIELD, FACES, SEND)
        scratch = [
            pltpu.VMEM((13, FACE, 128), F32),
            pltpu.VMEM((1600, 128), F32),
            pltpu.VMEM((1600, 128), F32),
            pltpu.VMEM((10, 160, 256), BF16),
            pltpu.VMEM((10, 160, 256), BF16),
        ]
        if last:
            scratch.append(pltpu.VMEM((1024, 128), F32))
        return pl.pallas_call(
            functools.partial(layer_kernel, skip is not None, last, index),
            out_shape=out_shape,
            in_specs=[SM, SM, SM] + [VM] * (len(args) - 3),
            out_specs=(VM,) * len(out_shape),
            scratch_shapes=scratch,
            compiler_params=params,
            name=f"layer{index}",
        )(*args)

    for index in range(0, convs, 2):
        inner = layer(index, field, faces, send, None, False)
        outer = layer(index + 1, *inner, field, index + 2 == convs)
        if index + 2 < convs:
            field, faces, send = outer
    return outer[0]


def solution(mesh):
    in_specs = (
        P(("space", "slab"), None, None, None),
        P(("space", "slab")),
        P(("space", "slab"), None),
        P(("space", "slab"), None),
        P(),
        P(),
    )
    out_specs = P(("space", "slab"), None, None, None)
    return jax.shard_map(shards, mesh=mesh, in_specs=in_specs, out_specs=out_specs, check_vma=False)
```

```python
import functools

import jax
import jax.numpy as jnp
from jax import lax
from jax.experimental import pallas as pl
from jax.experimental.pallas import tpu as pltpu
from jax.sharding import PartitionSpec as P

BRICK = 4
FACE = 192
PACK = 152
MIB = 1 << 20
VM = pl.BlockSpec(memory_space=pltpu.VMEM)
SM = pl.BlockSpec(memory_space=pltpu.SMEM)
HB = pl.BlockSpec(memory_space=pltpu.HBM)
F32, BF16 = jnp.float32, jnp.bfloat16
ORDER = [0, 3, 2, 1]
PLACE, SECOND, LIVE = 104, 108, 109


def direction(dx, dy, dz):
    at = (dx + 1) * 9 + (dy + 1) * 3 + dz + 1
    return at - (at > 13)


def lower_half(shape):
    return lax.broadcasted_iota(jnp.int32, shape, len(shape) - 1) < 64


def write_faces(field, faces):
    low = lower_half((8, 128))
    for b in range(2):
        for s in range(2):
            for i in range(8):
                col = (7 * s * 8 + i) * 8 + 4 * b
                faces[b, 32 * s + 4 * i : 32 * s + 4 * i + 4, :] = field[col : col + 4, :]
                col = (i * 8 + 7 * s) * 8 + 4 * b
                at = 64 + 32 * s + 4 * i
                faces[b, at : at + 4, :] = field[col : col + 4, :]
        for x in range(8):
            first = field[pl.ds(x * 64 + 4 * b, 8, stride=8), :]
            last = field[pl.ds(x * 64 + 4 * b + 3, 8, stride=8), :]
            faces[b, 128 + 8 * x : 136 + 8 * x, :] = jnp.where(low, first, last)


def offer(second, faces, send):
    for e, b in ((0, 0), (1, second)):
        send[e, 0:64, :] = faces[b, 0:64, :]
        for s in range(2):
            send[e, 64 + 24 * s : 88 + 24 * s, :] = faces[b, 68 + 32 * s : 92 + 32 * s, :]
        for x in range(6):
            at = 128 + 8 * (x + 1) + 1
            send[e, 112 + 6 * x : 118 + 6 * x, :] = faces[b, at : at + 6, :]
        send[e, 148:152, :] = jnp.zeros((4, 128), F32)


def unpack(pack, e, table, t):
    low = lower_half((8, 128))
    table[t, 0:64, :] = pack[e, 0:64, :]
    for s in range(2):
        table[t, 68 + 32 * s : 92 + 32 * s, :] = pack[e, 64 + 24 * s : 88 + 24 * s, :]
        for x in range(2):
            at = 64 + 32 * s + 28 * x
            table[t, at : at + 4, :] = pack[e, 32 * x + 28 * s : 32 * x + 28 * s + 4, :]
    for x in range(6):
        at = 128 + 8 * (x + 1) + 1
        table[t, at : at + 6, :] = pack[e, 112 + 6 * x : 118 + 6 * x, :]
    for s in range(2):
        first = table[t, pl.ds(64 + 32 * s, 8, stride=4), :]
        last = table[t, pl.ds(64 + 32 * s + 3, 8, stride=4), :]
        table[t, pl.ds(128 + 7 * s, 8, stride=8), :] = jnp.where(low, first, last)
        first = table[t, pl.ds(32 * s, 8, stride=4), :]
        last = table[t, pl.ds(32 * s + 3, 8, stride=4), :]
        table[t, 128 + 56 * s : 136 + 56 * s, :] = jnp.where(low, first, last)


def places_of(s0, s1):
    p0 = s0
    p1 = jnp.where(s1 == s0, (s0 + 1) % BRICK, s1)

    def free(slot):
        return (p0 != slot) & (p1 != slot)

    p2 = jnp.where(free(0), 0, jnp.where(free(1), 1, 2))
    return p0, p1, p2, 6 - p0 - p1 - p2


def enter(pair, live, slots, feat, field, faces, own, picked, sems):
    pick = pltpu.make_async_copy(slots, picked, sems.at[0])
    pick.start()
    copy = pltpu.make_async_copy(feat, own, sems.at[1])
    copy.start()
    pick.wait()
    places = places_of(picked[0, 0], picked[0, 1])
    copy.wait()
    for b in range(2):
        place = places[2 * pair + b]
        keep = jnp.where(place < live[0], 1.0, 0.0).astype(F32)
        for x in range(8):
            for q in range(4):
                tile = own[place, x, :, 128 * q : 128 * q + 128] * keep
                field[pl.ds(x * 64 + 4 * b + q, 8, stride=8), :] = tile
    write_faces(field, faces)


def entry_kernel(live, slots, feat, field, faces, send, own, picked, sems):
    enter(0, live, slots, feat, field, faces, own, picked, sems)
    offer(jnp.where(picked[0, 0] == picked[0, 1], 0, 1), faces, send)


def second_entry_kernel(
    after, live, slots, feat, weights, neighbours, field, faces, held, scalars, own, picked, sems, nbr, far
):
    fetch = pltpu.make_async_copy(weights, held, far.at[0])
    look = pltpu.make_async_copy(neighbours, nbr, far.at[1])
    fetch.start()
    look.start()
    enter(1, live, slots, feat, field, faces, own, picked, sems)
    look.wait()
    places = places_of(picked[0, 0], picked[0, 1])
    turns = [jnp.where(lax.axis_index(axis) % 2 == 0, 2, 0) for axis in ("space", "slab")]

    def rename(at, carry):
        for b in range(BRICK):
            t = nbr[b, at]
            new = jnp.where(t < 8, t ^ turns[0], jnp.where(t < 12, t ^ turns[1], t))
            for k in range(BRICK):
                new = jnp.where(t == places[k], k, new)
            scalars[26 * b + at] = new
        return carry

    lax.fori_loop(0, 26, rename, 0)
    for k in range(BRICK):
        scalars[PLACE + k] = places[k]
    scalars[SECOND] = jnp.where(picked[0, 0] == picked[0, 1], 0, 1)
    scalars[LIVE] = live[0]
    fetch.wait()


def make_taps(index, plain, taps, wide):
    low = lower_half((32, 128))
    zero = jnp.zeros((32, 128), F32)
    for t in range(9):
        even = [plain[pl.ds((3 * t + d) * 128 + index, 32, stride=4), :] for d in range(3)]
        odd = [pltpu.roll(rows, 64, 1) for rows in even]

        def rows(held, d):
            return held[d] if 0 <= d <= 2 else zero

        for w, base in ((0, 192), (1, 0), (2, 64), (3, 128)):
            wide[t % 2, pl.ds(base, 32, stride=2), :] = jnp.where(low, rows(even, w), rows(odd, w - 1))
            wide[t % 2, pl.ds(base + 1, 32, stride=2), :] = jnp.where(low, rows(odd, w), rows(even, w - 1))
        full = wide[t % 2]
        high = full.astype(BF16)
        taps[t, :, 0:128] = high
        taps[t, :, 128:256] = (full - high.astype(F32)).astype(BF16)


def first_taps_kernel(weights, plain, taps, wide):
    for t in range(27):
        for i in range(32):
            plain[128 * t + 4 * i : 128 * t + 4 * i + 4, :] = weights[t, :, 128 * i : 128 * i + 128]
    make_taps(0, plain, taps, wide)


def taps_kernel(index, after, plain, taps, wide):
    make_taps(index, plain, taps, wide)


def fill_table(faces, arrived, table):
    for k, ref in enumerate(faces):
        table[2 * k : 2 * k + 2] = ref[...]
    for k, ref in zip(ORDER, arrived):
        for e in range(2):
            unpack(ref, e, table, 4 + 2 * k + e)
    table[12] = jnp.zeros((FACE, 128), F32)


def fill_margins(pair, scalars, field, table, one, two):
    for x in range(8):
        one[(x + 1) * 80 + 8 : (x + 1) * 80 + 72, :] = field[x * 64 : x * 64 + 64, :]
    for b in range(2):
        near = 26 * scalars[PLACE + 2 * pair + b]

        def cell(xp, yp):
            return (xp * 10 + yp) * 8 + 4 * b

        for d in (-1, 1):
            s, p = (1, 0) if d < 0 else (0, 9)
            t = scalars[near + direction(d, 0, 0)]
            for i in range(8):
                at = cell(p, i + 1)
                one[at : at + 4, :] = table[t, 32 * s + 4 * i : 32 * s + 4 * i + 4, :]
            t = scalars[near + direction(0, d, 0)]
            for i in range(8):
                at = cell(i + 1, p)
                one[at : at + 4, :] = table[t, 64 + 32 * s + 4 * i : 64 + 32 * s + 4 * i + 4, :]
            for e in (-1, 1):
                y, py = (7, 0) if e < 0 else (0, 9)
                t = scalars[near + direction(d, e, 0)]
                at = cell(p, py)
                one[at : at + 4, :] = table[t, 32 * s + 4 * y : 32 * s + 4 * y + 4, :]
    low3 = lower_half((10, 8, 128))
    for c in range(10):
        rows = one[c * 80 : c * 80 + 80, :].reshape(10, 8, 128)
        both = jnp.where(low3, pltpu.roll(rows, 7, 1), pltpu.roll(rows, 1, 1))
        two[c * 80 : c * 80 + 80, :] = both.reshape(80, 128)
    low = lower_half((8, 128))
    low1 = lower_half((1, 128))
    for b in range(2):
        near = 26 * scalars[PLACE + 2 * pair + b]
        for dz in (-1, 1):
            def merge(start, stride, new):
                at = pl.ds(start, 8, stride=stride)
                old = two[at, :]
                two[at, :] = jnp.where(low, new, old) if dz > 0 else jnp.where(low, old, new)

            row = 4 * b + (3 if dz > 0 else 0)
            t = scalars[near + direction(0, 0, dz)]
            for x in range(8):
                merge(((x + 1) * 10 + 1) * 8 + row, 8, table[t, 128 + 8 * x : 136 + 8 * x, :])
            for d in (-1, 1):
                x, p = (7, 0) if d < 0 else (0, 9)
                t = scalars[near + direction(d, 0, dz)]
                merge((p * 10 + 1) * 8 + row, 8, table[t, 128 + 8 * x : 136 + 8 * x, :])
                t = scalars[near + direction(0, d, dz)]
                merge((10 + p) * 8 + row, 80, table[t, pl.ds(128 + x, 8, stride=8), :])
                for e in (-1, 1):
                    y, py = (7, 0) if e < 0 else (0, 9)
                    t = scalars[near + direction(d, e, dz)]
                    at = (p * 10 + py) * 8 + row
                    new = table[t, 128 + 8 * x + y : 129 + 8 * x + y, :]
                    old = two[at : at + 1, :]
                    two[at : at + 1, :] = jnp.where(low1, new, old) if dz > 0 else jnp.where(low1, old, new)


def split(one, two, high, rest, mid_high, mid_rest):
    for c in range(10):
        for half, ref in enumerate((one, two)):
            lanes = slice(128 * half, 128 * half + 128)
            full = ref[c * 80 : c * 80 + 80, :]
            top = full.astype(BF16)
            high[c, :, lanes] = top
            rest[c, :, lanes] = (full - top.astype(F32)).astype(BF16)
            full = ref[c * 80 + 8 : c * 80 + 72, :]
            top = full.astype(BF16)
            mid_high[c, :, lanes] = top
            mid_rest[c, :, lanes] = (full - top.astype(F32)).astype(BF16)


def convolve(high, rest, mid_high, mid_rest, taps):
    def rows(ref, mid, dx, dy):
        if dy == 1:
            return mid[dx : dx + 8].reshape(512, 256)
        return ref[dx : dx + 8, 8 * dy : 8 * dy + 64, :].reshape(512, 256)

    wide = None
    narrow = None
    for dx in range(3):
        for dy in range(3):
            kernel = taps[3 * dx + dy]
            part = jnp.dot(rows(high, mid_high, dx, dy), kernel, preferred_element_type=F32)
            wide = part if wide is None else wide + part
            part = jnp.dot(rows(rest, mid_rest, dx, dy), kernel[:, 0:128], preferred_element_type=F32)
            narrow = part if narrow is None else narrow + part
    return wide[:, 0:128] + (wide[:, 128:256] + narrow)


def run_pair(pair, index, scalars, field, table, taps, biases, skip, new, work):
    one, two, high, rest, mid_high, mid_rest = work
    fill_margins(pair, scalars, field, table, one, two)
    split(one, two, high, rest, mid_high, mid_rest)
    total = convolve(high, rest, mid_high, mid_rest, taps)
    bias = biases[index : index + 1, :]
    total = total + jnp.concatenate([bias, bias], 1)
    if skip is not None:
        total = total + skip[...]
    second = lax.broadcasted_iota(jnp.int32, (512, 128), 0) % 8 >= 4
    slot = jnp.where(second, scalars[PLACE + 2 * pair + 1], scalars[PLACE + 2 * pair])
    new[...] = jnp.where(slot < scalars[LIVE], jnp.maximum(total, 0.0), 0.0)


def near_kernel(residual, index, scalars, field, faces_a, faces_b, *refs):
    arrived, (taps, biases), refs = refs[:4], refs[4:6], refs[6:]
    skip, refs = (refs[0], refs[1:]) if residual else (None, refs)
    new, faces, send, table = refs[:4]
    fill_table((faces_a, faces_b), arrived, table)
    run_pair(0, index, scalars, field, table, taps, biases, skip, new, refs[4:])
    write_faces(new, faces)
    offer(scalars[SECOND], faces, send)


def far_kernel(residual, index, scalars, field, table, taps, biases, *refs):
    skip, refs = (refs[0], refs[1:]) if residual else (None, refs)
    new, faces = refs[:2]
    run_pair(1, index, scalars, field, table, taps, biases, skip, new, refs[2:])
    write_faces(new, faces)


def last_kernel(index, scalars, field_a, field_b, faces_a, faces_b, *refs):
    arrived, (taps, biases, skip_a, skip_b, out, table, new, stage, sems), work = refs[:4], refs[4:13], refs[13:]
    fill_table((faces_a, faces_b), arrived, table)
    copies = []
    for pair, field, skip in ((0, field_a, skip_a), (1, field_b, skip_b)):
        run_pair(pair, index, scalars, field, table, taps, biases, skip, new, work)
        for b in range(2):
            at = 2 * pair + b
            for x in range(8):
                for q in range(4):
                    stage[at, x, :, 128 * q : 128 * q + 128] = new[pl.ds(x * 64 + 4 * b + q, 8, stride=8), :]
            copies.append(pltpu.make_async_copy(stage.at[at], out.at[scalars[PLACE + at]], sems.at[at]))
            copies[-1].start()
    for copy in copies:
        copy.wait()


FIELD = jax.ShapeDtypeStruct((512, 128), F32)
FACES = jax.ShapeDtypeStruct((2, FACE, 128), F32)
SEND = jax.ShapeDtypeStruct((2, PACK, 128), F32)
TABLE = jax.ShapeDtypeStruct((13, FACE, 128), F32)
WORK = [
    pltpu.VMEM((800, 128), F32),
    pltpu.VMEM((800, 128), F32),
    pltpu.VMEM((10, 80, 256), BF16),
    pltpu.VMEM((10, 80, 256), BF16),
    pltpu.VMEM((10, 64, 256), BF16),
    pltpu.VMEM((10, 64, 256), BF16),
]


def swaps(size, first):
    pairs = [(i, i + 1) for i in range(first, size - 1, 2)]
    return pairs + [(b, a) for a, b in pairs]


def exchange(send):
    got = []
    for axis in ("space", "slab"):
        size = lax.axis_size(axis)
        got += [lax.ppermute(send, axis, swaps(size, first)) for first in (0, 1)]
    return [got[at] for at in ORDER]


def shards(features, live, rim_slots, neighbours, weights, biases):
    params = pltpu.CompilerParams(vmem_limit_bytes=24 * MIB)
    cost = pl.CostEstimate(flops=600_000_000, bytes_accessed=4 * MIB, transcendentals=0)
    convs = weights.shape[0]
    in_hbm = lambda array: pltpu.with_memory_space_constraint(array, pltpu.HBM)

    def call(kernel, name, out_shape, in_specs, scratch, args, out_specs=None):
        return pl.pallas_call(
            kernel,
            out_shape=out_shape,
            in_specs=in_specs,
            out_specs=tuple(VM for _ in out_shape) if out_specs is None else out_specs,
            scratch_shapes=scratch,
            compiler_params=params,
            cost_estimate=cost,
            name=name,
        )(*args)

    entry_scratch = [
        pltpu.VMEM(features.shape, F32),
        pltpu.SMEM((1, 2), jnp.int32),
        pltpu.SemaphoreType.DMA((2,)),
    ]
    field_a, faces_a, send = call(
        entry_kernel, "entry", (FIELD, FACES, SEND), [SM, HB, HB], entry_scratch,
        (live, in_hbm(rim_slots), in_hbm(features)),
    )
    turned = jnp.transpose(weights, (1, 0, 2))
    field_b, faces_b, held, scalars = call(
        second_entry_kernel,
        "second_entry",
        (FIELD, FACES, jax.ShapeDtypeStruct(turned.shape, F32), jax.ShapeDtypeStruct((LIVE + 1,), jnp.int32)),
        [pl.BlockSpec(memory_space=pl.ANY), SM, HB, HB, HB, HB],
        entry_scratch + [pltpu.SMEM(neighbours.shape, jnp.int32), pltpu.SemaphoreType.DMA((2,))],
        (send, live, in_hbm(rim_slots), in_hbm(features), in_hbm(turned), in_hbm(neighbours)),
        (VM, VM, VM, SM),
    )
    plain = None

    def taps_of(index, send):
        nonlocal plain
        shape = jax.ShapeDtypeStruct((9, 256, 256), BF16)
        scratch = [pltpu.VMEM((2, 256, 128), F32)]
        if index == 0:
            wide = jax.ShapeDtypeStruct((27 * 32 * convs, 128), F32)
            plain, taps = call(first_taps_kernel, "taps0", (wide, shape), [VM], scratch, (held,))
            return taps
        kernel = functools.partial(taps_kernel, index)
        specs = [pl.BlockSpec(memory_space=pl.ANY), VM]
        return call(kernel, f"taps{index}", (shape,), specs, scratch, (send, plain))[0]

    def layer(index, fields, faces, send, skips):
        arrived = exchange(send)
        taps = taps_of(index, send)
        args = [scalars, fields[0], *faces, *arrived, taps, biases]
        if skips is not None:
            args.append(skips[0])
        kernel = functools.partial(near_kernel, skips is not None, index)
        specs = [SM] + [VM] * (len(args) - 1)
        new_a, faces_a, send, table = call(
            kernel, f"near{index}", (FIELD, FACES, SEND, TABLE), specs, WORK, args
        )
        args = [scalars, fields[1], table, taps, biases]
        if skips is not None:
            args.append(skips[1])
        kernel = functools.partial(far_kernel, skips is not None, index)
        specs = [SM] + [VM] * (len(args) - 1)
        new_b, faces_b = call(kernel, f"far{index}", (FIELD, FACES), specs, WORK, args)
        return (new_a, new_b), (faces_a, faces_b), send

    def finish(index, fields, faces, send, skips):
        arrived = exchange(send)
        taps = taps_of(index, send)
        args = [scalars, *fields, *faces, *arrived, taps, biases, *skips]
        scratch = [
            pltpu.VMEM(TABLE.shape, F32),
            pltpu.VMEM(FIELD.shape, F32),
            pltpu.VMEM(features.shape, F32),
            pltpu.SemaphoreType.DMA((BRICK,)),
        ]
        out = (jax.ShapeDtypeStruct(features.shape, F32),)
        kernel = functools.partial(last_kernel, index)
        specs = [SM] + [VM] * (len(args) - 1)
        return call(kernel, f"last{index}", out, specs, scratch + WORK, args, (HB,))[0]

    state = (field_a, field_b), (faces_a, faces_b), send
    for index in range(0, convs, 2):
        skips = state[0]
        state = layer(index, *state, None)
        if index + 2 == convs:
            return finish(index + 1, *state, skips)
        state = layer(index + 1, *state, skips)


def solution(mesh):
    in_specs = (
        P(("space", "slab"), None, None, None),
        P(("space", "slab")),
        P(("space", "slab"), None),
        P(("space", "slab"), None),
        P(),
        P(),
    )
    out_specs = P(("space", "slab"), None, None, None)
    return jax.shard_map(shards, mesh=mesh, in_specs=in_specs, out_specs=out_specs, check_vma=False)
```

```python
import functools

import jax
import jax.numpy as jnp
from jax import lax
from jax.experimental import pallas as pl
from jax.experimental.pallas import tpu as pltpu
from jax.sharding import PartitionSpec as P

BRICK = 4
FACE = 192
PACK = 152
MIB = 1 << 20
VM = pl.BlockSpec(memory_space=pltpu.VMEM)
SM = pl.BlockSpec(memory_space=pltpu.SMEM)
HB = pl.BlockSpec(memory_space=pltpu.HBM)
F32, BF16 = jnp.float32, jnp.bfloat16
ORDER = [0, 3, 2, 1]
PLACE, SECOND, LIVE = 104, 108, 109


def direction(dx, dy, dz):
    at = (dx + 1) * 9 + (dy + 1) * 3 + dz + 1
    return at - (at > 13)


def lower_half(shape):
    return lax.broadcasted_iota(jnp.int32, shape, len(shape) - 1) < 64


def write_faces(field, faces):
    low = lower_half((8, 128))
    for b in range(2):
        for s in range(2):
            for i in range(8):
                col = (7 * s * 8 + i) * 8 + 4 * b
                faces[b, 32 * s + 4 * i : 32 * s + 4 * i + 4, :] = field[col : col + 4, :]
                col = (i * 8 + 7 * s) * 8 + 4 * b
                at = 64 + 32 * s + 4 * i
                faces[b, at : at + 4, :] = field[col : col + 4, :]
        for x in range(8):
            first = field[pl.ds(x * 64 + 4 * b, 8, stride=8), :]
            last = field[pl.ds(x * 64 + 4 * b + 3, 8, stride=8), :]
            faces[b, 128 + 8 * x : 136 + 8 * x, :] = jnp.where(low, first, last)


def offer(second, faces, send):
    for e, b in ((0, 0), (1, second)):
        send[e, 0:64, :] = faces[b, 0:64, :]
        for s in range(2):
            send[e, 64 + 24 * s : 88 + 24 * s, :] = faces[b, 68 + 32 * s : 92 + 32 * s, :]
        for x in range(6):
            at = 128 + 8 * (x + 1) + 1
            send[e, 112 + 6 * x : 118 + 6 * x, :] = faces[b, at : at + 6, :]
        send[e, 148:152, :] = jnp.zeros((4, 128), F32)


def unpack(pack, e, table, t):
    low = lower_half((8, 128))
    table[t, 0:64, :] = pack[e, 0:64, :]
    for s in range(2):
        table[t, 68 + 32 * s : 92 + 32 * s, :] = pack[e, 64 + 24 * s : 88 + 24 * s, :]
        for x in range(2):
            at = 64 + 32 * s + 28 * x
            table[t, at : at + 4, :] = pack[e, 32 * x + 28 * s : 32 * x + 28 * s + 4, :]
    for x in range(6):
        at = 128 + 8 * (x + 1) + 1
        table[t, at : at + 6, :] = pack[e, 112 + 6 * x : 118 + 6 * x, :]
    for s in range(2):
        first = table[t, pl.ds(64 + 32 * s, 8, stride=4), :]
        last = table[t, pl.ds(64 + 32 * s + 3, 8, stride=4), :]
        table[t, pl.ds(128 + 7 * s, 8, stride=8), :] = jnp.where(low, first, last)
        first = table[t, pl.ds(32 * s, 8, stride=4), :]
        last = table[t, pl.ds(32 * s + 3, 8, stride=4), :]
        table[t, 128 + 56 * s : 136 + 56 * s, :] = jnp.where(low, first, last)


def places_of(s0, s1):
    p0 = s0
    p1 = jnp.where(s1 == s0, (s0 + 1) % BRICK, s1)

    def free(slot):
        return (p0 != slot) & (p1 != slot)

    p2 = jnp.where(free(0), 0, jnp.where(free(1), 1, 2))
    return p0, p1, p2, 6 - p0 - p1 - p2


def enter(pair, live, slots, feat, field, faces, own, picked, sems):
    pick = pltpu.make_async_copy(slots, picked, sems.at[0])
    pick.start()
    copy = pltpu.make_async_copy(feat, own, sems.at[1])
    copy.start()
    pick.wait()
    places = places_of(picked[0, 0], picked[0, 1])
    copy.wait()
    for b in range(2):
        place = places[2 * pair + b]
        keep = jnp.where(place < live[0], 1.0, 0.0).astype(F32)
        for x in range(8):
            for q in range(4):
                tile = own[place, x, :, 128 * q : 128 * q + 128] * keep
                field[pl.ds(x * 64 + 4 * b + q, 8, stride=8), :] = tile
    write_faces(field, faces)


def entry_kernel(live, slots, feat, field, faces, send, own, picked, sems):
    enter(0, live, slots, feat, field, faces, own, picked, sems)
    offer(jnp.where(picked[0, 0] == picked[0, 1], 0, 1), faces, send)


def second_entry_kernel(
    after, live, slots, feat, weights, neighbours, field, faces, held, scalars, own, picked, sems, nbr, far
):
    fetch = pltpu.make_async_copy(weights, held, far.at[0])
    look = pltpu.make_async_copy(neighbours, nbr, far.at[1])
    fetch.start()
    look.start()
    enter(1, live, slots, feat, field, faces, own, picked, sems)
    look.wait()
    places = places_of(picked[0, 0], picked[0, 1])
    turns = [jnp.where(lax.axis_index(axis) % 2 == 0, 2, 0) for axis in ("space", "slab")]

    def rename(at, carry):
        for b in range(BRICK):
            t = nbr[b, at]
            new = jnp.where(t < 8, t ^ turns[0], jnp.where(t < 12, t ^ turns[1], t))
            for k in range(BRICK):
                new = jnp.where(t == places[k], k, new)
            scalars[26 * b + at] = new
        return carry

    lax.fori_loop(0, 26, rename, 0)
    for k in range(BRICK):
        scalars[PLACE + k] = places[k]
    scalars[SECOND] = jnp.where(picked[0, 0] == picked[0, 1], 0, 1)
    scalars[LIVE] = live[0]
    fetch.wait()


def make_taps(index, plain, taps, wide):
    low = lower_half((32, 128))
    zero = jnp.zeros((32, 128), F32)
    for t in range(9):
        even = [plain[pl.ds((3 * t + d) * 128 + index, 32, stride=4), :] for d in range(3)]
        odd = [pltpu.roll(rows, 64, 1) for rows in even]

        def rows(held, d):
            return held[d] if 0 <= d <= 2 else zero

        for w, base in ((0, 192), (1, 0), (2, 64), (3, 128)):
            wide[t % 2, pl.ds(base, 32, stride=2), :] = jnp.where(low, rows(even, w), rows(odd, w - 1))
            wide[t % 2, pl.ds(base + 1, 32, stride=2), :] = jnp.where(low, rows(odd, w), rows(even, w - 1))
        full = wide[t % 2]
        high = full.astype(BF16)
        taps[t, :, 0:128] = high
        taps[t, :, 128:256] = (full - high.astype(F32)).astype(BF16)


def first_taps_kernel(weights, plain, taps, wide):
    for t in range(27):
        for i in range(32):
            plain[128 * t + 4 * i : 128 * t + 4 * i + 4, :] = weights[t, :, 128 * i : 128 * i + 128]
    make_taps(0, plain, taps, wide)


def taps_kernel(index, after, plain, taps, wide):
    make_taps(index, plain, taps, wide)


def fill_table(faces, arrived, table):
    for k, ref in enumerate(faces):
        table[2 * k : 2 * k + 2] = ref[...]
    for k, ref in zip(ORDER, arrived):
        for e in range(2):
            unpack(ref, e, table, 4 + 2 * k + e)
    table[12] = jnp.zeros((FACE, 128), F32)


def fill_margins(pair, scalars, field, table, one, two):
    for x in range(8):
        one[(x + 1) * 80 + 8 : (x + 1) * 80 + 72, :] = field[x * 64 : x * 64 + 64, :]
    for b in range(2):
        near = 26 * scalars[PLACE + 2 * pair + b]

        def cell(xp, yp):
            return (xp * 10 + yp) * 8 + 4 * b

        for d in (-1, 1):
            s, p = (1, 0) if d < 0 else (0, 9)
            t = scalars[near + direction(d, 0, 0)]
            for i in range(8):
                at = cell(p, i + 1)
                one[at : at + 4, :] = table[t, 32 * s + 4 * i : 32 * s + 4 * i + 4, :]
            t = scalars[near + direction(0, d, 0)]
            for i in range(8):
                at = cell(i + 1, p)
                one[at : at + 4, :] = table[t, 64 + 32 * s + 4 * i : 64 + 32 * s + 4 * i + 4, :]
            for e in (-1, 1):
                y, py = (7, 0) if e < 0 else (0, 9)
                t = scalars[near + direction(d, e, 0)]
                at = cell(p, py)
                one[at : at + 4, :] = table[t, 32 * s + 4 * y : 32 * s + 4 * y + 4, :]
    low3 = lower_half((10, 8, 128))
    for c in range(10):
        rows = one[c * 80 : c * 80 + 80, :].reshape(10, 8, 128)
        both = jnp.where(low3, pltpu.roll(rows, 7, 1), pltpu.roll(rows, 1, 1))
        two[c * 80 : c * 80 + 80, :] = both.reshape(80, 128)
    low = lower_half((8, 128))
    low1 = lower_half((1, 128))
    for b in range(2):
        near = 26 * scalars[PLACE + 2 * pair + b]
        for dz in (-1, 1):
            def merge(start, stride, new):
                at = pl.ds(start, 8, stride=stride)
                old = two[at, :]
                two[at, :] = jnp.where(low, new, old) if dz > 0 else jnp.where(low, old, new)

            row = 4 * b + (3 if dz > 0 else 0)
            t = scalars[near + direction(0, 0, dz)]
            for x in range(8):
                merge(((x + 1) * 10 + 1) * 8 + row, 8, table[t, 128 + 8 * x : 136 + 8 * x, :])
            for d in (-1, 1):
                x, p = (7, 0) if d < 0 else (0, 9)
                t = scalars[near + direction(d, 0, dz)]
                merge((p * 10 + 1) * 8 + row, 8, table[t, 128 + 8 * x : 136 + 8 * x, :])
                t = scalars[near + direction(0, d, dz)]
                merge((10 + p) * 8 + row, 80, table[t, pl.ds(128 + x, 8, stride=8), :])
                for e in (-1, 1):
                    y, py = (7, 0) if e < 0 else (0, 9)
                    t = scalars[near + direction(d, e, dz)]
                    at = (p * 10 + py) * 8 + row
                    new = table[t, 128 + 8 * x + y : 129 + 8 * x + y, :]
                    old = two[at : at + 1, :]
                    two[at : at + 1, :] = jnp.where(low1, new, old) if dz > 0 else jnp.where(low1, old, new)


def split(one, two, high, rest, mid_high, mid_rest):
    for c in range(10):
        for half, ref in enumerate((one, two)):
            lanes = slice(128 * half, 128 * half + 128)
            full = ref[c * 80 : c * 80 + 80, :]
            top = full.astype(BF16)
            high[c, :, lanes] = top
            rest[c, :, lanes] = (full - top.astype(F32)).astype(BF16)
            full = ref[c * 80 + 8 : c * 80 + 72, :]
            top = full.astype(BF16)
            mid_high[c, :, lanes] = top
            mid_rest[c, :, lanes] = (full - top.astype(F32)).astype(BF16)


def convolve(high, rest, mid_high, mid_rest, taps):
    def rows(ref, mid, dx, dy, planes=8):
        if dy == 1:
            return mid[dx : dx + planes].reshape(64 * planes, 256)
        return ref[dx : dx + planes, 8 * dy : 8 * dy + 64, :].reshape(64 * planes, 256)

    def product(left, right):
        return jnp.dot(left, right, preferred_element_type=F32)

    wide = None
    for dx in range(3):
        for dy in range(3):
            part = product(rows(high, mid_high, dx, dy), taps[3 * dx + dy])
            wide = part if wide is None else wide + part
    total = wide[:, 0:128] + wide[:, 128:256]
    for dy in range(3):
        two = jnp.concatenate([taps[dy, :, 0:128], taps[3 + dy, :, 0:128]], 1)
        part = product(rows(rest, mid_rest, 0, dy, 9), two)
        total = total + (part[0:512, 0:128] + part[64:576, 128:256])
    two = jnp.concatenate([taps[6, :, 0:128], taps[7, :, 0:128]], 1)
    part = product(rest[2:10].reshape(640, 256), two).reshape(8, 80, 256)
    total = total + (part[:, 0:64, 0:128] + part[:, 8:72, 128:256]).reshape(512, 128)
    return total + product(rows(rest, mid_rest, 2, 2), taps[8, :, 0:128])


def run_pair(pair, index, scalars, field, table, taps, biases, skip, new, work):
    one, two, high, rest, mid_high, mid_rest = work
    fill_margins(pair, scalars, field, table, one, two)
    split(one, two, high, rest, mid_high, mid_rest)
    total = convolve(high, rest, mid_high, mid_rest, taps)
    bias = biases[index : index + 1, :]
    total = total + jnp.concatenate([bias, bias], 1)
    if skip is not None:
        total = total + skip[...]
    second = lax.broadcasted_iota(jnp.int32, (512, 128), 0) % 8 >= 4
    slot = jnp.where(second, scalars[PLACE + 2 * pair + 1], scalars[PLACE + 2 * pair])
    new[...] = jnp.where(slot < scalars[LIVE], jnp.maximum(total, 0.0), 0.0)


def near_kernel(residual, index, scalars, field, faces_a, faces_b, *refs):
    arrived, (taps, biases), refs = refs[:4], refs[4:6], refs[6:]
    skip, refs = (refs[0], refs[1:]) if residual else (None, refs)
    new, faces, send, table = refs[:4]
    fill_table((faces_a, faces_b), arrived, table)
    run_pair(0, index, scalars, field, table, taps, biases, skip, new, refs[4:])
    write_faces(new, faces)
    offer(scalars[SECOND], faces, send)


def far_kernel(residual, index, scalars, field, table, taps, biases, *refs):
    skip, refs = (refs[0], refs[1:]) if residual else (None, refs)
    new, faces = refs[:2]
    run_pair(1, index, scalars, field, table, taps, biases, skip, new, refs[2:])
    write_faces(new, faces)


def last_kernel(index, scalars, field_a, field_b, faces_a, faces_b, *refs):
    arrived, (taps, biases, skip_a, skip_b, out, table, new_a, new_b, stage, sems), work = refs[:4], refs[4:14], refs[14:]
    fill_table((faces_a, faces_b), arrived, table)
    copies = []
    for pair, field, skip, new in ((0, field_a, skip_a, new_a), (1, field_b, skip_b, new_b)):
        own = work[6 * pair : 6 * pair + 6]
        run_pair(pair, index, scalars, field, table, taps, biases, skip, new, own)
        for b in range(2):
            at = 2 * pair + b
            for x in range(8):
                for q in range(4):
                    stage[at, x, :, 128 * q : 128 * q + 128] = new[pl.ds(x * 64 + 4 * b + q, 8, stride=8), :]
            copies.append(pltpu.make_async_copy(stage.at[at], out.at[scalars[PLACE + at]], sems.at[at]))
            copies[-1].start()
    for copy in copies:
        copy.wait()


FIELD = jax.ShapeDtypeStruct((512, 128), F32)
FACES = jax.ShapeDtypeStruct((2, FACE, 128), F32)
SEND = jax.ShapeDtypeStruct((2, PACK, 128), F32)
TABLE = jax.ShapeDtypeStruct((13, FACE, 128), F32)
WORK = [
    pltpu.VMEM((800, 128), F32),
    pltpu.VMEM((800, 128), F32),
    pltpu.VMEM((10, 80, 256), BF16),
    pltpu.VMEM((10, 80, 256), BF16),
    pltpu.VMEM((10, 64, 256), BF16),
    pltpu.VMEM((10, 64, 256), BF16),
]


def swaps(size, first):
    pairs = [(i, i + 1) for i in range(first, size - 1, 2)]
    return pairs + [(b, a) for a, b in pairs]


def exchange(send):
    got = []
    for axis in ("space", "slab"):
        size = lax.axis_size(axis)
        got += [lax.ppermute(send, axis, swaps(size, first)) for first in (0, 1)]
    return [got[at] for at in ORDER]


def shards(features, live, rim_slots, neighbours, weights, biases):
    params = pltpu.CompilerParams(vmem_limit_bytes=24 * MIB)
    cost = pl.CostEstimate(flops=600_000_000, bytes_accessed=4 * MIB, transcendentals=0)
    convs = weights.shape[0]
    in_hbm = lambda array: pltpu.with_memory_space_constraint(array, pltpu.HBM)

    def call(kernel, name, out_shape, in_specs, scratch, args, out_specs=None):
        return pl.pallas_call(
            kernel,
            out_shape=out_shape,
            in_specs=in_specs,
            out_specs=tuple(VM for _ in out_shape) if out_specs is None else out_specs,
            scratch_shapes=scratch,
            compiler_params=params,
            cost_estimate=cost,
            name=name,
        )(*args)

    entry_scratch = [
        pltpu.VMEM(features.shape, F32),
        pltpu.SMEM((1, 2), jnp.int32),
        pltpu.SemaphoreType.DMA((2,)),
    ]
    field_a, faces_a, send = call(
        entry_kernel, "entry", (FIELD, FACES, SEND), [SM, HB, HB], entry_scratch,
        (live, in_hbm(rim_slots), in_hbm(features)),
    )
    turned = jnp.transpose(weights, (1, 0, 2))
    field_b, faces_b, held, scalars = call(
        second_entry_kernel,
        "second_entry",
        (FIELD, FACES, jax.ShapeDtypeStruct(turned.shape, F32), pltpu.SMEM((LIVE + 1,), jnp.int32)),
        [pl.BlockSpec(memory_space=pl.ANY), SM, HB, HB, HB, HB],
        entry_scratch + [pltpu.SMEM(neighbours.shape, jnp.int32), pltpu.SemaphoreType.DMA((2,))],
        (send, live, in_hbm(rim_slots), in_hbm(features), in_hbm(turned), in_hbm(neighbours)),
        (VM, VM, VM, SM),
    )
    plain = None

    def taps_of(index, send):
        nonlocal plain
        shape = jax.ShapeDtypeStruct((9, 256, 256), BF16)
        scratch = [pltpu.VMEM((2, 256, 128), F32)]
        if index == 0:
            wide = jax.ShapeDtypeStruct((27 * 32 * convs, 128), F32)
            plain, taps = call(first_taps_kernel, "taps0", (wide, shape), [VM], scratch, (held,))
            return taps
        kernel = functools.partial(taps_kernel, index)
        specs = [pl.BlockSpec(memory_space=pl.ANY), VM]
        return call(kernel, f"taps{index}", (shape,), specs, scratch, (send, plain))[0]

    def layer(index, fields, faces, send, skips):
        arrived = exchange(send)
        taps = taps_of(index, send)
        args = [scalars, fields[0], *faces, *arrived, taps, biases]
        if skips is not None:
            args.append(skips[0])
        kernel = functools.partial(near_kernel, skips is not None, index)
        specs = [SM] + [VM] * (len(args) - 1)
        new_a, faces_a, send, table = call(
            kernel, f"near{index}", (FIELD, FACES, SEND, TABLE), specs, WORK, args
        )
        args = [scalars, fields[1], table, taps, biases]
        if skips is not None:
            args.append(skips[1])
        kernel = functools.partial(far_kernel, skips is not None, index)
        specs = [SM] + [VM] * (len(args) - 1)
        new_b, faces_b = call(kernel, f"far{index}", (FIELD, FACES), specs, WORK, args)
        return (new_a, new_b), (faces_a, faces_b), send

    def finish(index, fields, faces, send, skips):
        arrived = exchange(send)
        taps = taps_of(index, send)
        args = [scalars, *fields, *faces, *arrived, taps, biases, *skips]
        scratch = [
            pltpu.VMEM(TABLE.shape, F32),
            pltpu.VMEM(FIELD.shape, F32),
            pltpu.VMEM(FIELD.shape, F32),
            pltpu.VMEM(features.shape, F32),
            pltpu.SemaphoreType.DMA((BRICK,)),
        ]
        out = (jax.ShapeDtypeStruct(features.shape, F32),)
        kernel = functools.partial(last_kernel, index)
        specs = [SM] + [VM] * (len(args) - 1)
        return call(kernel, f"last{index}", out, specs, scratch + WORK + WORK, args, (HB,))[0]

    state = (field_a, field_b), (faces_a, faces_b), send
    for index in range(0, convs, 2):
        skips = state[0]
        state = layer(index, *state, None)
        if index + 2 == convs:
            return finish(index + 1, *state, skips)
        state = layer(index + 1, *state, skips)


def solution(mesh):
    in_specs = (
        P(("space", "slab"), None, None, None),
        P(("space", "slab")),
        P(("space", "slab"), None),
        P(("space", "slab"), None),
        P(),
        P(),
    )
    out_specs = P(("space", "slab"), None, None, None)
    return jax.shard_map(shards, mesh=mesh, in_specs=in_specs, out_specs=out_specs, check_vma=False)
```

```python
import functools

import jax
import jax.numpy as jnp
from jax import lax
from jax.experimental import pallas as pl
from jax.experimental.pallas import tpu as pltpu
from jax.sharding import PartitionSpec as P

BRICK = 4
FACE = 192
PACK = 152
MIB = 1 << 20
VM = pl.BlockSpec(memory_space=pltpu.VMEM)
SM = pl.BlockSpec(memory_space=pltpu.SMEM)
HB = pl.BlockSpec(memory_space=pltpu.HBM)
F32, BF16 = jnp.float32, jnp.bfloat16
ORDER = [0, 3, 2, 1]
PLACE, SECOND, LIVE = 104, 108, 109


def direction(dx, dy, dz):
    at = (dx + 1) * 9 + (dy + 1) * 3 + dz + 1
    return at - (at > 13)


def lower_half(shape):
    return lax.broadcasted_iota(jnp.int32, shape, len(shape) - 1) < 64


def write_faces(field, faces):
    low = lower_half((8, 128))
    for b in range(2):
        for s in range(2):
            for i in range(8):
                col = (7 * s * 8 + i) * 8 + 4 * b
                faces[b, 32 * s + 4 * i : 32 * s + 4 * i + 4, :] = field[col : col + 4, :]
                col = (i * 8 + 7 * s) * 8 + 4 * b
                at = 64 + 32 * s + 4 * i
                faces[b, at : at + 4, :] = field[col : col + 4, :]
        for x in range(8):
            first = field[pl.ds(x * 64 + 4 * b, 8, stride=8), :]
            last = field[pl.ds(x * 64 + 4 * b + 3, 8, stride=8), :]
            faces[b, 128 + 8 * x : 136 + 8 * x, :] = jnp.where(low, first, last)


def offer(second, faces, send):
    for e, b in ((0, 0), (1, second)):
        send[e, 0:64, :] = faces[b, 0:64, :]
        for s in range(2):
            send[e, 64 + 24 * s : 88 + 24 * s, :] = faces[b, 68 + 32 * s : 92 + 32 * s, :]
        for x in range(6):
            at = 128 + 8 * (x + 1) + 1
            send[e, 112 + 6 * x : 118 + 6 * x, :] = faces[b, at : at + 6, :]
        send[e, 148:152, :] = jnp.zeros((4, 128), F32)


def unpack(pack, e, table, t):
    low = lower_half((8, 128))
    table[t, 0:64, :] = pack[e, 0:64, :]
    for s in range(2):
        table[t, 68 + 32 * s : 92 + 32 * s, :] = pack[e, 64 + 24 * s : 88 + 24 * s, :]
        for x in range(2):
            at = 64 + 32 * s + 28 * x
            table[t, at : at + 4, :] = pack[e, 32 * x + 28 * s : 32 * x + 28 * s + 4, :]
    for x in range(6):
        at = 128 + 8 * (x + 1) + 1
        table[t, at : at + 6, :] = pack[e, 112 + 6 * x : 118 + 6 * x, :]
    for s in range(2):
        first = table[t, pl.ds(64 + 32 * s, 8, stride=4), :]
        last = table[t, pl.ds(64 + 32 * s + 3, 8, stride=4), :]
        table[t, pl.ds(128 + 7 * s, 8, stride=8), :] = jnp.where(low, first, last)
        first = table[t, pl.ds(32 * s, 8, stride=4), :]
        last = table[t, pl.ds(32 * s + 3, 8, stride=4), :]
        table[t, 128 + 56 * s : 136 + 56 * s, :] = jnp.where(low, first, last)


def places_of(s0, s1):
    p0 = s0
    p1 = jnp.where(s1 == s0, (s0 + 1) % BRICK, s1)

    def free(slot):
        return (p0 != slot) & (p1 != slot)

    p2 = jnp.where(free(0), 0, jnp.where(free(1), 1, 2))
    return p0, p1, p2, 6 - p0 - p1 - p2


def enter(pair, live, slots, feat, field, faces, own, picked, sems):
    pick = pltpu.make_async_copy(slots, picked, sems.at[0])
    pick.start()
    copy = pltpu.make_async_copy(feat, own, sems.at[1])
    copy.start()
    pick.wait()
    places = places_of(picked[0, 0], picked[0, 1])
    copy.wait()
    for b in range(2):
        place = places[2 * pair + b]
        keep = jnp.where(place < live[0], 1.0, 0.0).astype(F32)
        for x in range(8):
            for q in range(4):
                tile = own[place, x, :, 128 * q : 128 * q + 128] * keep
                field[pl.ds(x * 64 + 4 * b + q, 8, stride=8), :] = tile
    write_faces(field, faces)


def entry_kernel(live, slots, feat, field, faces, send, own, picked, sems):
    enter(0, live, slots, feat, field, faces, own, picked, sems)
    offer(jnp.where(picked[0, 0] == picked[0, 1], 0, 1), faces, send)


def second_entry_kernel(
    after, live, slots, feat, weights, neighbours, field, faces, held, scalars, own, picked, sems, nbr, far
):
    fetch = pltpu.make_async_copy(weights, held, far.at[0])
    look = pltpu.make_async_copy(neighbours, nbr, far.at[1])
    fetch.start()
    look.start()
    enter(1, live, slots, feat, field, faces, own, picked, sems)
    look.wait()
    places = places_of(picked[0, 0], picked[0, 1])
    turns = [jnp.where(lax.axis_index(axis) % 2 == 0, 2, 0) for axis in ("space", "slab")]
    ends = [(lax.axis_index(axis), lax.axis_size(axis) - 1) for axis in ("space", "slab")]

    def rename(at, carry):
        for b in range(BRICK):
            t = nbr[b, at]
            new = jnp.where(t < 8, t ^ turns[0], jnp.where(t < 12, t ^ turns[1], t))
            for k, (place, end) in enumerate(ends):
                side = (t - 4 - 4 * k) // 2
                new = jnp.where(((side == 0) & (place == 0)) | ((side == 1) & (place == end)), 12, new)
            for k in range(BRICK):
                new = jnp.where(t == places[k], k, new)
            scalars[26 * b + at] = new
        return carry

    lax.fori_loop(0, 26, rename, 0)
    for k in range(BRICK):
        scalars[PLACE + k] = places[k]
    scalars[SECOND] = jnp.where(picked[0, 0] == picked[0, 1], 0, 1)
    scalars[LIVE] = live[0]
    fetch.wait()


def make_taps(index, plain, taps, wide):
    low = lower_half((32, 128))
    zero = jnp.zeros((32, 128), F32)
    for t in range(9):
        even = [plain[pl.ds((3 * t + d) * 128 + index, 32, stride=4), :] for d in range(3)]
        odd = [pltpu.roll(rows, 64, 1) for rows in even]

        def rows(held, d):
            return held[d] if 0 <= d <= 2 else zero

        for w, base in ((0, 192), (1, 0), (2, 64), (3, 128)):
            wide[t % 2, pl.ds(base, 32, stride=2), :] = jnp.where(low, rows(even, w), rows(odd, w - 1))
            wide[t % 2, pl.ds(base + 1, 32, stride=2), :] = jnp.where(low, rows(odd, w), rows(even, w - 1))
        full = wide[t % 2]
        high = full.astype(BF16)
        taps[t, :, 0:128] = high
        taps[t, :, 128:256] = (full - high.astype(F32)).astype(BF16)


def first_taps_kernel(weights, plain, taps, wide):
    for t in range(27):
        for i in range(32):
            plain[128 * t + 4 * i : 128 * t + 4 * i + 4, :] = weights[t, :, 128 * i : 128 * i + 128]
    make_taps(0, plain, taps, wide)


def taps_kernel(index, after, plain, taps, wide):
    make_taps(index, plain, taps, wide)


def fill_table(faces, arrived, table):
    for k, ref in enumerate(faces):
        table[2 * k : 2 * k + 2] = ref[...]
    for k, ref in zip(ORDER, arrived):
        for e in range(2):
            unpack(ref, e, table, 4 + 2 * k + e)
    table[12] = jnp.zeros((FACE, 128), F32)


def fill_margins(pair, scalars, field, table, one, two):
    for x in range(8):
        one[(x + 1) * 80 + 8 : (x + 1) * 80 + 72, :] = field[x * 64 : x * 64 + 64, :]
    for b in range(2):
        near = 26 * scalars[PLACE + 2 * pair + b]

        def cell(xp, yp):
            return (xp * 10 + yp) * 8 + 4 * b

        for d in (-1, 1):
            s, p = (1, 0) if d < 0 else (0, 9)
            t = scalars[near + direction(d, 0, 0)]
            for i in range(8):
                at = cell(p, i + 1)
                one[at : at + 4, :] = table[t, 32 * s + 4 * i : 32 * s + 4 * i + 4, :]
            t = scalars[near + direction(0, d, 0)]
            for i in range(8):
                at = cell(i + 1, p)
                one[at : at + 4, :] = table[t, 64 + 32 * s + 4 * i : 64 + 32 * s + 4 * i + 4, :]
            for e in (-1, 1):
                y, py = (7, 0) if e < 0 else (0, 9)
                t = scalars[near + direction(d, e, 0)]
                at = cell(p, py)
                one[at : at + 4, :] = table[t, 32 * s + 4 * y : 32 * s + 4 * y + 4, :]
    low3 = lower_half((10, 8, 128))
    for c in range(10):
        rows = one[c * 80 : c * 80 + 80, :].reshape(10, 8, 128)
        both = jnp.where(low3, pltpu.roll(rows, 7, 1), pltpu.roll(rows, 1, 1))
        two[c * 80 : c * 80 + 80, :] = both.reshape(80, 128)
    low = lower_half((8, 128))
    low1 = lower_half((1, 128))
    for b in range(2):
        near = 26 * scalars[PLACE + 2 * pair + b]
        for dz in (-1, 1):
            def merge(start, stride, new):
                at = pl.ds(start, 8, stride=stride)
                old = two[at, :]
                two[at, :] = jnp.where(low, new, old) if dz > 0 else jnp.where(low, old, new)

            row = 4 * b + (3 if dz > 0 else 0)
            t = scalars[near + direction(0, 0, dz)]
            for x in range(8):
                merge(((x + 1) * 10 + 1) * 8 + row, 8, table[t, 128 + 8 * x : 136 + 8 * x, :])
            for d in (-1, 1):
                x, p = (7, 0) if d < 0 else (0, 9)
                t = scalars[near + direction(d, 0, dz)]
                merge((p * 10 + 1) * 8 + row, 8, table[t, 128 + 8 * x : 136 + 8 * x, :])
                t = scalars[near + direction(0, d, dz)]
                merge((10 + p) * 8 + row, 80, table[t, pl.ds(128 + x, 8, stride=8), :])
                for e in (-1, 1):
                    y, py = (7, 0) if e < 0 else (0, 9)
                    t = scalars[near + direction(d, e, dz)]
                    at = (p * 10 + py) * 8 + row
                    new = table[t, 128 + 8 * x + y : 129 + 8 * x + y, :]
                    old = two[at : at + 1, :]
                    two[at : at + 1, :] = jnp.where(low1, new, old) if dz > 0 else jnp.where(low1, old, new)


def split(one, two, high, rest, mid_high, mid_rest):
    for c in range(10):
        for half, ref in enumerate((one, two)):
            lanes = slice(128 * half, 128 * half + 128)
            full = ref[c * 80 : c * 80 + 80, :]
            top = full.astype(BF16)
            high[c, :, lanes] = top
            rest[c, :, lanes] = (full - top.astype(F32)).astype(BF16)
            full = ref[c * 80 + 8 : c * 80 + 72, :]
            top = full.astype(BF16)
            mid_high[c, :, lanes] = top
            mid_rest[c, :, lanes] = (full - top.astype(F32)).astype(BF16)


def convolve(high, rest, mid_high, mid_rest, taps):
    def rows(ref, mid, dx, dy, planes=8):
        if dy == 1:
            return mid[dx : dx + planes].reshape(64 * planes, 256)
        return ref[dx : dx + planes, 8 * dy : 8 * dy + 64, :].reshape(64 * planes, 256)

    def product(left, right):
        return jnp.dot(left, right, preferred_element_type=F32)

    wide = None
    for dx in range(3):
        for dy in range(3):
            part = product(rows(high, mid_high, dx, dy), taps[3 * dx + dy])
            wide = part if wide is None else wide + part
    total = wide[:, 0:128] + wide[:, 128:256]
    for dy in range(3):
        two = jnp.concatenate([taps[dy, :, 0:128], taps[3 + dy, :, 0:128]], 1)
        part = product(rows(rest, mid_rest, 0, dy, 9), two)
        total = total + (part[0:512, 0:128] + part[64:576, 128:256])
    two = jnp.concatenate([taps[6, :, 0:128], taps[7, :, 0:128]], 1)
    part = product(rest[2:10].reshape(640, 256), two).reshape(8, 80, 256)
    total = total + (part[:, 0:64, 0:128] + part[:, 8:72, 128:256]).reshape(512, 128)
    return total + product(rows(rest, mid_rest, 2, 2), taps[8, :, 0:128])


def run_pair(pair, index, scalars, field, table, taps, biases, skip, new, work):
    one, two, high, rest, mid_high, mid_rest = work
    fill_margins(pair, scalars, field, table, one, two)
    split(one, two, high, rest, mid_high, mid_rest)
    total = convolve(high, rest, mid_high, mid_rest, taps)
    bias = biases[index : index + 1, :]
    total = total + jnp.concatenate([bias, bias], 1)
    if skip is not None:
        total = total + skip[...]
    second = lax.broadcasted_iota(jnp.int32, (512, 128), 0) % 8 >= 4
    slot = jnp.where(second, scalars[PLACE + 2 * pair + 1], scalars[PLACE + 2 * pair])
    new[...] = jnp.where(slot < scalars[LIVE], jnp.maximum(total, 0.0), 0.0)


def near_kernel(residual, index, scalars, field, faces_a, faces_b, *refs):
    arrived, (taps, biases), refs = refs[:4], refs[4:6], refs[6:]
    skip, refs = (refs[0], refs[1:]) if residual else (None, refs)
    new, faces, send, table = refs[:4]
    fill_table((faces_a, faces_b), arrived, table)
    run_pair(0, index, scalars, field, table, taps, biases, skip, new, refs[4:])
    write_faces(new, faces)
    offer(scalars[SECOND], faces, send)


def far_kernel(residual, index, scalars, field, table, taps, biases, *refs):
    skip, refs = (refs[0], refs[1:]) if residual else (None, refs)
    new, faces = refs[:2]
    run_pair(1, index, scalars, field, table, taps, biases, skip, new, refs[2:])
    write_faces(new, faces)


def last_kernel(index, scalars, field_a, field_b, faces_a, faces_b, *refs):
    arrived, (taps, biases, skip_a, skip_b, out, table, new_a, new_b, stage, sems), work = refs[:4], refs[4:14], refs[14:]
    fill_table((faces_a, faces_b), arrived, table)
    copies = []
    for pair, field, skip, new in ((0, field_a, skip_a, new_a), (1, field_b, skip_b, new_b)):
        own = work[6 * pair : 6 * pair + 6]
        run_pair(pair, index, scalars, field, table, taps, biases, skip, new, own)
        for b in range(2):
            at = 2 * pair + b
            for x in range(8):
                for q in range(4):
                    stage[at, x, :, 128 * q : 128 * q + 128] = new[pl.ds(x * 64 + 4 * b + q, 8, stride=8), :]
            copies.append(pltpu.make_async_copy(stage.at[at], out.at[scalars[PLACE + at]], sems.at[at]))
            copies[-1].start()
    for copy in copies:
        copy.wait()


FIELD = jax.ShapeDtypeStruct((512, 128), F32)
FACES = jax.ShapeDtypeStruct((2, FACE, 128), F32)
SEND = jax.ShapeDtypeStruct((2, PACK, 128), F32)
TABLE = jax.ShapeDtypeStruct((13, FACE, 128), F32)
WORK = [
    pltpu.VMEM((800, 128), F32),
    pltpu.VMEM((800, 128), F32),
    pltpu.VMEM((10, 80, 256), BF16),
    pltpu.VMEM((10, 80, 256), BF16),
    pltpu.VMEM((10, 64, 256), BF16),
    pltpu.VMEM((10, 64, 256), BF16),
]


def swaps(size, first):
    pairs = [(i, (i + 1) % size) for i in range(first, size, 2)]
    return pairs + [(b, a) for a, b in pairs]


def exchange(send):
    got = []
    for axis in ("space", "slab"):
        size = lax.axis_size(axis)
        got += [lax.ppermute(send, axis, swaps(size, first)) for first in (0, 1)]
    return [got[at] for at in ORDER]


def shards(features, live, rim_slots, neighbours, weights, biases):
    params = pltpu.CompilerParams(vmem_limit_bytes=24 * MIB)
    cost = pl.CostEstimate(flops=600_000_000, bytes_accessed=4 * MIB, transcendentals=0)
    convs = weights.shape[0]
    in_hbm = lambda array: pltpu.with_memory_space_constraint(array, pltpu.HBM)

    def call(kernel, name, out_shape, in_specs, scratch, args, out_specs=None):
        return pl.pallas_call(
            kernel,
            out_shape=out_shape,
            in_specs=in_specs,
            out_specs=tuple(VM for _ in out_shape) if out_specs is None else out_specs,
            scratch_shapes=scratch,
            compiler_params=params,
            cost_estimate=cost,
            name=name,
        )(*args)

    entry_scratch = [
        pltpu.VMEM(features.shape, F32),
        pltpu.SMEM((1, 2), jnp.int32),
        pltpu.SemaphoreType.DMA((2,)),
    ]
    field_a, faces_a, send = call(
        entry_kernel, "entry", (FIELD, FACES, SEND), [SM, HB, HB], entry_scratch,
        (live, in_hbm(rim_slots), in_hbm(features)),
    )
    turned = jnp.transpose(weights, (1, 0, 2))
    field_b, faces_b, held, scalars = call(
        second_entry_kernel,
        "second_entry",
        (FIELD, FACES, jax.ShapeDtypeStruct(turned.shape, F32), pltpu.SMEM((LIVE + 1,), jnp.int32)),
        [pl.BlockSpec(memory_space=pl.ANY), SM, HB, HB, HB, HB],
        entry_scratch + [pltpu.SMEM(neighbours.shape, jnp.int32), pltpu.SemaphoreType.DMA((2,))],
        (send, live, in_hbm(rim_slots), in_hbm(features), in_hbm(turned), in_hbm(neighbours)),
        (VM, VM, VM, SM),
    )
    plain = None

    def taps_of(index, send):
        nonlocal plain
        shape = jax.ShapeDtypeStruct((9, 256, 256), BF16)
        scratch = [pltpu.VMEM((2, 256, 128), F32)]
        if index == 0:
            wide = jax.ShapeDtypeStruct((27 * 32 * convs, 128), F32)
            plain, taps = call(first_taps_kernel, "taps0", (wide, shape), [VM], scratch, (held,))
            return taps
        kernel = functools.partial(taps_kernel, index)
        specs = [pl.BlockSpec(memory_space=pl.ANY), VM]
        return call(kernel, f"taps{index}", (shape,), specs, scratch, (send, plain))[0]

    def layer(index, fields, faces, send, skips):
        arrived = exchange(send)
        taps = taps_of(index, send)
        args = [scalars, fields[0], *faces, *arrived, taps, biases]
        if skips is not None:
            args.append(skips[0])
        kernel = functools.partial(near_kernel, skips is not None, index)
        specs = [SM] + [VM] * (len(args) - 1)
        new_a, faces_a, send, table = call(
            kernel, f"near{index}", (FIELD, FACES, SEND, TABLE), specs, WORK, args
        )
        args = [scalars, fields[1], table, taps, biases]
        if skips is not None:
            args.append(skips[1])
        kernel = functools.partial(far_kernel, skips is not None, index)
        specs = [SM] + [VM] * (len(args) - 1)
        new_b, faces_b = call(kernel, f"far{index}", (FIELD, FACES), specs, WORK, args)
        return (new_a, new_b), (faces_a, faces_b), send

    def finish(index, fields, faces, send, skips):
        arrived = exchange(send)
        taps = taps_of(index, send)
        args = [scalars, *fields, *faces, *arrived, taps, biases, *skips]
        scratch = [
            pltpu.VMEM(TABLE.shape, F32),
            pltpu.VMEM(FIELD.shape, F32),
            pltpu.VMEM(FIELD.shape, F32),
            pltpu.VMEM(features.shape, F32),
            pltpu.SemaphoreType.DMA((BRICK,)),
        ]
        out = (jax.ShapeDtypeStruct(features.shape, F32),)
        kernel = functools.partial(last_kernel, index)
        specs = [SM] + [VM] * (len(args) - 1)
        return call(kernel, f"last{index}", out, specs, scratch + WORK + WORK, args, (HB,))[0]

    state = (field_a, field_b), (faces_a, faces_b), send
    for index in range(0, convs, 2):
        skips = state[0]
        state = layer(index, *state, None)
        if index + 2 == convs:
            return finish(index + 1, *state, skips)
        state = layer(index + 1, *state, skips)


def solution(mesh):
    in_specs = (
        P(("space", "slab"), None, None, None),
        P(("space", "slab")),
        P(("space", "slab"), None),
        P(("space", "slab"), None),
        P(),
        P(),
    )
    out_specs = P(("space", "slab"), None, None, None)
    return jax.shard_map(shards, mesh=mesh, in_specs=in_specs, out_specs=out_specs, check_vma=False)
```

```python
import functools

import jax
import jax.numpy as jnp
from jax import lax
from jax.experimental import pallas as pl
from jax.experimental.pallas import tpu as pltpu
from jax.sharding import PartitionSpec as P

BRICK = 4
FACE = 192
PACK = 152
MIB = 1 << 20
VM = pl.BlockSpec(memory_space=pltpu.VMEM)
SM = pl.BlockSpec(memory_space=pltpu.SMEM)
HB = pl.BlockSpec(memory_space=pltpu.HBM)
F32, BF16 = jnp.float32, jnp.bfloat16
ORDER = [0, 3, 2, 1]
PLACE, SECOND, LIVE = 0, 4, 5


def direction(dx, dy, dz):
    at = (dx + 1) * 9 + (dy + 1) * 3 + dz + 1
    return at - (at > 13)


def lower_half(shape):
    return lax.broadcasted_iota(jnp.int32, shape, len(shape) - 1) < 64


def write_faces(field, faces):
    low = lower_half((8, 128))
    for b in range(2):
        for s in range(2):
            for i in range(8):
                col = (7 * s * 8 + i) * 8 + 4 * b
                faces[b, 32 * s + 4 * i : 32 * s + 4 * i + 4, :] = field[col : col + 4, :]
                col = (i * 8 + 7 * s) * 8 + 4 * b
                at = 64 + 32 * s + 4 * i
                faces[b, at : at + 4, :] = field[col : col + 4, :]
        for x in range(8):
            first = field[pl.ds(x * 64 + 4 * b, 8, stride=8), :]
            last = field[pl.ds(x * 64 + 4 * b + 3, 8, stride=8), :]
            faces[b, 128 + 8 * x : 136 + 8 * x, :] = jnp.where(low, first, last)


def offer(second, faces, send):
    for e, b in ((0, 0), (1, second)):
        send[e, 0:64, :] = faces[b, 0:64, :]
        for s in range(2):
            send[e, 64 + 24 * s : 88 + 24 * s, :] = faces[b, 68 + 32 * s : 92 + 32 * s, :]
        for x in range(6):
            at = 128 + 8 * (x + 1) + 1
            send[e, 112 + 6 * x : 118 + 6 * x, :] = faces[b, at : at + 6, :]
        send[e, 148:152, :] = jnp.zeros((4, 128), F32)


def unpack(pack, e, table, t):
    low = lower_half((8, 128))
    table[t, 0:64, :] = pack[e, 0:64, :]
    for s in range(2):
        table[t, 68 + 32 * s : 92 + 32 * s, :] = pack[e, 64 + 24 * s : 88 + 24 * s, :]
        for x in range(2):
            at = 64 + 32 * s + 28 * x
            table[t, at : at + 4, :] = pack[e, 32 * x + 28 * s : 32 * x + 28 * s + 4, :]
    for x in range(6):
        at = 128 + 8 * (x + 1) + 1
        table[t, at : at + 6, :] = pack[e, 112 + 6 * x : 118 + 6 * x, :]
    for s in range(2):
        first = table[t, pl.ds(64 + 32 * s, 8, stride=4), :]
        last = table[t, pl.ds(64 + 32 * s + 3, 8, stride=4), :]
        table[t, pl.ds(128 + 7 * s, 8, stride=8), :] = jnp.where(low, first, last)
        first = table[t, pl.ds(32 * s, 8, stride=4), :]
        last = table[t, pl.ds(32 * s + 3, 8, stride=4), :]
        table[t, 128 + 56 * s : 136 + 56 * s, :] = jnp.where(low, first, last)


def places_of(s0, s1):
    p0 = s0
    p1 = jnp.where(s1 == s0, (s0 + 1) % BRICK, s1)

    def free(slot):
        return (p0 != slot) & (p1 != slot)

    p2 = jnp.where(free(0), 0, jnp.where(free(1), 1, 2))
    return p0, p1, p2, 6 - p0 - p1 - p2


def enter(pair, live, slots, feat, field, faces, own, picked, sems):
    pick = pltpu.make_async_copy(slots, picked, sems.at[0])
    pick.start()
    copy = pltpu.make_async_copy(feat, own, sems.at[1])
    copy.start()
    pick.wait()
    places = places_of(picked[0, 0], picked[0, 1])
    copy.wait()
    for b in range(2):
        place = places[2 * pair + b]
        keep = jnp.where(place < live[0], 1.0, 0.0).astype(F32)
        for x in range(8):
            for q in range(4):
                tile = own[place, x, :, 128 * q : 128 * q + 128] * keep
                field[pl.ds(x * 64 + 4 * b + q, 8, stride=8), :] = tile
    write_faces(field, faces)


def entry_kernel(live, slots, feat, field, faces, send, own, picked, sems):
    enter(0, live, slots, feat, field, faces, own, picked, sems)
    offer(jnp.where(picked[0, 0] == picked[0, 1], 0, 1), faces, send)


def second_entry_kernel(
    after, live, slots, feat, weights, neighbours, field, faces, held, names, scalars, own, picked, sems, nbr, named, far
):
    look = pltpu.make_async_copy(neighbours, nbr, far.at[1])
    fetch = pltpu.make_async_copy(weights, held, far.at[0])
    look.start()
    fetch.start()
    enter(1, live, slots, feat, field, faces, own, picked, sems)
    places = places_of(picked[0, 0], picked[0, 1])
    look.wait()
    t = nbr[...]
    new = t
    for k in range(BRICK):
        new = jnp.where(t == places[k], k, new)
    for k, axis in enumerate(("space", "slab")):
        place = lax.axis_index(axis)
        turn = jnp.where(place % 2 == 0, 2, 0)
        low = jnp.where(place == 0, 12, 4 + 4 * k + turn)
        high = jnp.where(place == lax.axis_size(axis) - 1, 12, 6 + 4 * k - turn)
        for e in range(2):
            new = jnp.where(t == 4 + 4 * k + e, jnp.minimum(low + e, 12), new)
            new = jnp.where(t == 6 + 4 * k + e, jnp.minimum(high + e, 12), new)
    named[:, 0:26] = new
    hand = pltpu.make_async_copy(named, names, far.at[2])
    hand.start()
    for k in range(BRICK):
        scalars[PLACE + k] = places[k]
    scalars[SECOND] = jnp.where(picked[0, 0] == picked[0, 1], 0, 1)
    scalars[LIVE] = live[0]
    fetch.wait()
    hand.wait()


def make_taps(index, plain, taps, wide):
    low = lower_half((32, 128))
    zero = jnp.zeros((32, 128), F32)
    for t in range(9):
        even = [plain[pl.ds((3 * t + d) * 128 + index, 32, stride=4), :] for d in range(3)]
        odd = [pltpu.roll(rows, 64, 1) for rows in even]

        def rows(held, d):
            return held[d] if 0 <= d <= 2 else zero

        for w, base in ((0, 192), (1, 0), (2, 64), (3, 128)):
            wide[t % 2, pl.ds(base, 32, stride=2), :] = jnp.where(low, rows(even, w), rows(odd, w - 1))
            wide[t % 2, pl.ds(base + 1, 32, stride=2), :] = jnp.where(low, rows(odd, w), rows(even, w - 1))
        full = wide[t % 2]
        high = full.astype(BF16)
        taps[t, :, 0:128] = high
        taps[t, :, 128:256] = (full - high.astype(F32)).astype(BF16)


def first_taps_kernel(weights, plain, taps, wide):
    for t in range(27):
        for i in range(32):
            plain[128 * t + 4 * i : 128 * t + 4 * i + 4, :] = weights[t, :, 128 * i : 128 * i + 128]
    make_taps(0, plain, taps, wide)


def taps_kernel(index, after, plain, taps, wide):
    make_taps(index, plain, taps, wide)


def fill_table(faces, arrived, table):
    for k, ref in enumerate(faces):
        table[2 * k : 2 * k + 2] = ref[...]
    for k, ref in zip(ORDER, arrived):
        for e in range(2):
            unpack(ref, e, table, 4 + 2 * k + e)
    table[12] = jnp.zeros((FACE, 128), F32)


def fill_margins(pair, names, scalars, field, table, one, two):
    for x in range(8):
        one[(x + 1) * 80 + 8 : (x + 1) * 80 + 72, :] = field[x * 64 : x * 64 + 64, :]
    for b in range(2):
        near = scalars[PLACE + 2 * pair + b]

        def cell(xp, yp):
            return (xp * 10 + yp) * 8 + 4 * b

        for d in (-1, 1):
            s, p = (1, 0) if d < 0 else (0, 9)
            t = names[near, direction(d, 0, 0)]
            for i in range(8):
                at = cell(p, i + 1)
                one[at : at + 4, :] = table[t, 32 * s + 4 * i : 32 * s + 4 * i + 4, :]
            t = names[near, direction(0, d, 0)]
            for i in range(8):
                at = cell(i + 1, p)
                one[at : at + 4, :] = table[t, 64 + 32 * s + 4 * i : 64 + 32 * s + 4 * i + 4, :]
            for e in (-1, 1):
                y, py = (7, 0) if e < 0 else (0, 9)
                t = names[near, direction(d, e, 0)]
                at = cell(p, py)
                one[at : at + 4, :] = table[t, 32 * s + 4 * y : 32 * s + 4 * y + 4, :]
    low3 = lower_half((10, 8, 128))
    for c in range(10):
        rows = one[c * 80 : c * 80 + 80, :].reshape(10, 8, 128)
        both = jnp.where(low3, pltpu.roll(rows, 7, 1), pltpu.roll(rows, 1, 1))
        two[c * 80 : c * 80 + 80, :] = both.reshape(80, 128)
    low = lower_half((8, 128))
    low1 = lower_half((1, 128))
    for b in range(2):
        near = scalars[PLACE + 2 * pair + b]
        for dz in (-1, 1):
            def merge(start, stride, new):
                at = pl.ds(start, 8, stride=stride)
                old = two[at, :]
                two[at, :] = jnp.where(low, new, old) if dz > 0 else jnp.where(low, old, new)

            row = 4 * b + (3 if dz > 0 else 0)
            t = names[near, direction(0, 0, dz)]
            for x in range(8):
                merge(((x + 1) * 10 + 1) * 8 + row, 8, table[t, 128 + 8 * x : 136 + 8 * x, :])
            for d in (-1, 1):
                x, p = (7, 0) if d < 0 else (0, 9)
                t = names[near, direction(d, 0, dz)]
                merge((p * 10 + 1) * 8 + row, 8, table[t, 128 + 8 * x : 136 + 8 * x, :])
                t = names[near, direction(0, d, dz)]
                merge((10 + p) * 8 + row, 80, table[t, pl.ds(128 + x, 8, stride=8), :])
                for e in (-1, 1):
                    y, py = (7, 0) if e < 0 else (0, 9)
                    t = names[near, direction(d, e, dz)]
                    at = (p * 10 + py) * 8 + row
                    new = table[t, 128 + 8 * x + y : 129 + 8 * x + y, :]
                    old = two[at : at + 1, :]
                    two[at : at + 1, :] = jnp.where(low1, new, old) if dz > 0 else jnp.where(low1, old, new)


def split(one, two, high, rest, mid_high, mid_rest):
    for c in range(10):
        for half, ref in enumerate((one, two)):
            lanes = slice(128 * half, 128 * half + 128)
            full = ref[c * 80 : c * 80 + 80, :]
            top = full.astype(BF16)
            high[c, :, lanes] = top
            rest[c, :, lanes] = (full - top.astype(F32)).astype(BF16)
            full = ref[c * 80 + 8 : c * 80 + 72, :]
            top = full.astype(BF16)
            mid_high[c, :, lanes] = top
            mid_rest[c, :, lanes] = (full - top.astype(F32)).astype(BF16)


def convolve(high, rest, mid_high, mid_rest, taps):
    def rows(ref, mid, dx, dy, planes=8):
        if dy == 1:
            return mid[dx : dx + planes].reshape(64 * planes, 256)
        return ref[dx : dx + planes, 8 * dy : 8 * dy + 64, :].reshape(64 * planes, 256)

    def product(left, right):
        return jnp.dot(left, right, preferred_element_type=F32)

    wide = None
    for dx in range(3):
        for dy in range(3):
            part = product(rows(high, mid_high, dx, dy), taps[3 * dx + dy])
            wide = part if wide is None else wide + part
    total = wide[:, 0:128] + wide[:, 128:256]
    for dy in range(3):
        two = jnp.concatenate([taps[dy, :, 0:128], taps[3 + dy, :, 0:128]], 1)
        part = product(rows(rest, mid_rest, 0, dy, 9), two)
        total = total + (part[0:512, 0:128] + part[64:576, 128:256])
    two = jnp.concatenate([taps[6, :, 0:128], taps[7, :, 0:128]], 1)
    part = product(rest[2:10].reshape(640, 256), two).reshape(8, 80, 256)
    total = total + (part[:, 0:64, 0:128] + part[:, 8:72, 128:256]).reshape(512, 128)
    return total + product(rows(rest, mid_rest, 2, 2), taps[8, :, 0:128])


def run_pair(pair, index, names, scalars, field, table, taps, biases, skip, new, work):
    one, two, high, rest, mid_high, mid_rest = work
    fill_margins(pair, names, scalars, field, table, one, two)
    split(one, two, high, rest, mid_high, mid_rest)
    total = convolve(high, rest, mid_high, mid_rest, taps)
    bias = biases[index : index + 1, :]
    total = total + jnp.concatenate([bias, bias], 1)
    if skip is not None:
        total = total + skip[...]
    second = lax.broadcasted_iota(jnp.int32, (512, 128), 0) % 8 >= 4
    slot = jnp.where(second, scalars[PLACE + 2 * pair + 1], scalars[PLACE + 2 * pair])
    new[...] = jnp.where(slot < scalars[LIVE], jnp.maximum(total, 0.0), 0.0)


def near_kernel(residual, index, names, scalars, field, faces_a, faces_b, *refs):
    arrived, (taps, biases), refs = refs[:4], refs[4:6], refs[6:]
    skip, refs = (refs[0], refs[1:]) if residual else (None, refs)
    new, faces, send, table = refs[:4]
    fill_table((faces_a, faces_b), arrived, table)
    run_pair(0, index, names, scalars, field, table, taps, biases, skip, new, refs[4:])
    write_faces(new, faces)
    offer(scalars[SECOND], faces, send)


def far_kernel(residual, index, names, scalars, field, table, taps, biases, *refs):
    skip, refs = (refs[0], refs[1:]) if residual else (None, refs)
    new, faces = refs[:2]
    run_pair(1, index, names, scalars, field, table, taps, biases, skip, new, refs[2:])
    write_faces(new, faces)


def last_kernel(index, names, scalars, field_a, field_b, faces_a, faces_b, *refs):
    arrived, (taps, biases, skip_a, skip_b, out, table, new_a, new_b, stage, sems), work = refs[:4], refs[4:14], refs[14:]
    fill_table((faces_a, faces_b), arrived, table)
    copies = []
    for pair, field, skip, new in ((0, field_a, skip_a, new_a), (1, field_b, skip_b, new_b)):
        own = work[6 * pair : 6 * pair + 6]
        run_pair(pair, index, names, scalars, field, table, taps, biases, skip, new, own)
        for b in range(2):
            at = 2 * pair + b
            for x in range(8):
                for q in range(4):
                    stage[at, x, :, 128 * q : 128 * q + 128] = new[pl.ds(x * 64 + 4 * b + q, 8, stride=8), :]
            copies.append(pltpu.make_async_copy(stage.at[at], out.at[scalars[PLACE + at]], sems.at[at]))
            copies[-1].start()
    for copy in copies:
        copy.wait()


FIELD = jax.ShapeDtypeStruct((512, 128), F32)
FACES = jax.ShapeDtypeStruct((2, FACE, 128), F32)
SEND = jax.ShapeDtypeStruct((2, PACK, 128), F32)
TABLE = jax.ShapeDtypeStruct((13, FACE, 128), F32)
WORK = [
    pltpu.VMEM((800, 128), F32),
    pltpu.VMEM((800, 128), F32),
    pltpu.VMEM((10, 80, 256), BF16),
    pltpu.VMEM((10, 80, 256), BF16),
    pltpu.VMEM((10, 64, 256), BF16),
    pltpu.VMEM((10, 64, 256), BF16),
]


def swaps(along, first):
    spaces, slabs = lax.axis_size("space"), lax.axis_size("slab")
    pairs = []
    for space in range(spaces):
        for slab in range(slabs):
            place, size = ((space, spaces), (slab, slabs))[along]
            other = place + 1 if (place - first) % 2 == 0 else place - 1
            if 0 <= other < size:
                to = ((other, slab), (space, other))[along]
            else:
                to = ((space, slab ^ 1), (space ^ 1, slab))[along]
            pairs.append((space * slabs + slab, to[0] * slabs + to[1]))
    return pairs


def exchange(send):
    got = [lax.ppermute(send, ("space", "slab"), swaps(at // 2, at % 2)) for at in range(4)]
    return [got[at] for at in ORDER]


def shards(features, live, rim_slots, neighbours, weights, biases):
    params = pltpu.CompilerParams(vmem_limit_bytes=24 * MIB)
    cost = pl.CostEstimate(flops=600_000_000, bytes_accessed=4 * MIB, transcendentals=0)
    convs = weights.shape[0]
    in_hbm = lambda array: pltpu.with_memory_space_constraint(array, pltpu.HBM)

    def call(kernel, name, out_shape, in_specs, scratch, args, out_specs=None):
        return pl.pallas_call(
            kernel,
            out_shape=out_shape,
            in_specs=in_specs,
            out_specs=tuple(VM for _ in out_shape) if out_specs is None else out_specs,
            scratch_shapes=scratch,
            compiler_params=params,
            cost_estimate=cost,
            name=name,
        )(*args)

    entry_scratch = [
        pltpu.VMEM(features.shape, F32),
        pltpu.SMEM((1, 2), jnp.int32),
        pltpu.SemaphoreType.DMA((2,)),
    ]
    field_a, faces_a, send = call(
        entry_kernel, "entry", (FIELD, FACES, SEND), [SM, HB, HB], entry_scratch,
        (live, in_hbm(rim_slots), in_hbm(features)),
    )
    turned = jnp.transpose(weights, (1, 0, 2))
    field_b, faces_b, held, names, scalars = call(
        second_entry_kernel,
        "second_entry",
        (FIELD, FACES, jax.ShapeDtypeStruct(turned.shape, F32), pltpu.SMEM((BRICK, 128), jnp.int32), pltpu.SMEM((LIVE + 1,), jnp.int32)),
        [pl.BlockSpec(memory_space=pl.ANY), SM, HB, HB, HB, HB],
        entry_scratch
        + [
            pltpu.VMEM(neighbours.shape, jnp.int32),
            pltpu.VMEM((BRICK, 128), jnp.int32),
            pltpu.SemaphoreType.DMA((3,)),
        ],
        (send, live, in_hbm(rim_slots), in_hbm(features), in_hbm(turned), in_hbm(neighbours)),
        (VM, VM, VM, SM, SM),
    )
    plain = None

    def taps_of(index, send):
        nonlocal plain
        shape = jax.ShapeDtypeStruct((9, 256, 256), BF16)
        scratch = [pltpu.VMEM((2, 256, 128), F32)]
        if index == 0:
            wide = jax.ShapeDtypeStruct((27 * 32 * convs, 128), F32)
            plain, taps = call(first_taps_kernel, "taps0", (wide, shape), [VM], scratch, (held,))
            return taps
        kernel = functools.partial(taps_kernel, index)
        specs = [pl.BlockSpec(memory_space=pl.ANY), VM]
        return call(kernel, f"taps{index}", (shape,), specs, scratch, (send, plain))[0]

    def layer(index, fields, faces, send, skips):
        arrived = exchange(send)
        taps = taps_of(index, send)
        args = [names, scalars, fields[0], *faces, *arrived, taps, biases]
        if skips is not None:
            args.append(skips[0])
        kernel = functools.partial(near_kernel, skips is not None, index)
        specs = [SM, SM] + [VM] * (len(args) - 2)
        new_a, faces_a, send, table = call(
            kernel, f"near{index}", (FIELD, FACES, SEND, TABLE), specs, WORK, args
        )
        args = [names, scalars, fields[1], table, taps, biases]
        if skips is not None:
            args.append(skips[1])
        kernel = functools.partial(far_kernel, skips is not None, index)
        specs = [SM, SM] + [VM] * (len(args) - 2)
        new_b, faces_b = call(kernel, f"far{index}", (FIELD, FACES), specs, WORK, args)
        return (new_a, new_b), (faces_a, faces_b), send

    def finish(index, fields, faces, send, skips):
        arrived = exchange(send)
        taps = taps_of(index, send)
        args = [names, scalars, *fields, *faces, *arrived, taps, biases, *skips]
        scratch = [
            pltpu.VMEM(TABLE.shape, F32),
            pltpu.VMEM(FIELD.shape, F32),
            pltpu.VMEM(FIELD.shape, F32),
            pltpu.VMEM(features.shape, F32),
            pltpu.SemaphoreType.DMA((BRICK,)),
        ]
        out = (jax.ShapeDtypeStruct(features.shape, F32),)
        kernel = functools.partial(last_kernel, index)
        specs = [SM, SM] + [VM] * (len(args) - 2)
        return call(kernel, f"last{index}", out, specs, scratch + WORK + WORK, args, (HB,))[0]

    state = (field_a, field_b), (faces_a, faces_b), send
    for index in range(0, convs, 2):
        skips = state[0]
        state = layer(index, *state, None)
        if index + 2 == convs:
            return finish(index + 1, *state, skips)
        state = layer(index + 1, *state, skips)


def solution(mesh):
    in_specs = (
        P(("space", "slab"), None, None, None),
        P(("space", "slab")),
        P(("space", "slab"), None),
        P(("space", "slab"), None),
        P(),
        P(),
    )
    out_specs = P(("space", "slab"), None, None, None)
    return jax.shard_map(shards, mesh=mesh, in_specs=in_specs, out_specs=out_specs, check_vma=False)
```

```python
import functools

import jax
import jax.numpy as jnp
from jax import lax
from jax.experimental import pallas as pl
from jax.experimental.pallas import tpu as pltpu
from jax.sharding import PartitionSpec as P

BRICK = 4
FACE = 192
PACK = 152
MIB = 1 << 20
VM = pl.BlockSpec(memory_space=pltpu.VMEM)
SM = pl.BlockSpec(memory_space=pltpu.SMEM)
HB = pl.BlockSpec(memory_space=pltpu.HBM)
F32, BF16 = jnp.float32, jnp.bfloat16
ORDER = [0, 3, 1, 2]
PLACE, SECOND, LIVE = 0, 4, 5


def direction(dx, dy, dz):
    at = (dx + 1) * 9 + (dy + 1) * 3 + dz + 1
    return at - (at > 13)


def lower_half(shape):
    return lax.broadcasted_iota(jnp.int32, shape, len(shape) - 1) < 64


def write_faces(field, faces):
    low = lower_half((8, 128))
    for b in range(2):
        for s in range(2):
            for i in range(8):
                col = (7 * s * 8 + i) * 8 + 4 * b
                faces[b, 32 * s + 4 * i : 32 * s + 4 * i + 4, :] = field[col : col + 4, :]
                col = (i * 8 + 7 * s) * 8 + 4 * b
                at = 64 + 32 * s + 4 * i
                faces[b, at : at + 4, :] = field[col : col + 4, :]
        for x in range(8):
            first = field[pl.ds(x * 64 + 4 * b, 8, stride=8), :]
            last = field[pl.ds(x * 64 + 4 * b + 3, 8, stride=8), :]
            faces[b, 128 + 8 * x : 136 + 8 * x, :] = jnp.where(low, first, last)


def offer(second, faces, send):
    for e, b in ((0, 0), (1, second)):
        send[e, 0:64, :] = faces[b, 0:64, :]
        for s in range(2):
            send[e, 64 + 24 * s : 88 + 24 * s, :] = faces[b, 68 + 32 * s : 92 + 32 * s, :]
        for x in range(6):
            at = 128 + 8 * (x + 1) + 1
            send[e, 112 + 6 * x : 118 + 6 * x, :] = faces[b, at : at + 6, :]
        send[e, 148:152, :] = jnp.zeros((4, 128), F32)


def unpack(pack, e, table, t):
    low = lower_half((8, 128))
    table[t, 0:64, :] = pack[e, 0:64, :]
    for s in range(2):
        table[t, 68 + 32 * s : 92 + 32 * s, :] = pack[e, 64 + 24 * s : 88 + 24 * s, :]
        for x in range(2):
            at = 64 + 32 * s + 28 * x
            table[t, at : at + 4, :] = pack[e, 32 * x + 28 * s : 32 * x + 28 * s + 4, :]
    for x in range(6):
        at = 128 + 8 * (x + 1) + 1
        table[t, at : at + 6, :] = pack[e, 112 + 6 * x : 118 + 6 * x, :]
    for s in range(2):
        first = table[t, pl.ds(64 + 32 * s, 8, stride=4), :]
        last = table[t, pl.ds(64 + 32 * s + 3, 8, stride=4), :]
        table[t, pl.ds(128 + 7 * s, 8, stride=8), :] = jnp.where(low, first, last)
        first = table[t, pl.ds(32 * s, 8, stride=4), :]
        last = table[t, pl.ds(32 * s + 3, 8, stride=4), :]
        table[t, 128 + 56 * s : 136 + 56 * s, :] = jnp.where(low, first, last)


def places_of(s0, s1):
    p0 = s0
    p1 = jnp.where(s1 == s0, (s0 + 1) % BRICK, s1)

    def free(slot):
        return (p0 != slot) & (p1 != slot)

    p2 = jnp.where(free(0), 0, jnp.where(free(1), 1, 2))
    return p0, p1, p2, 6 - p0 - p1 - p2


def enter(pair, live, slots, feat, field, faces, own, picked, sems):
    pick = pltpu.make_async_copy(slots, picked, sems.at[0])
    pick.start()
    copy = pltpu.make_async_copy(feat, own, sems.at[1])
    copy.start()
    pick.wait()
    places = places_of(picked[0, 0], picked[0, 1])
    copy.wait()
    for b in range(2):
        place = places[2 * pair + b]
        keep = jnp.where(place < live[0], 1.0, 0.0).astype(F32)
        for x in range(8):
            for q in range(4):
                tile = own[place, x, :, 128 * q : 128 * q + 128] * keep
                field[pl.ds(x * 64 + 4 * b + q, 8, stride=8), :] = tile
    write_faces(field, faces)


def entry_kernel(live, slots, feat, field, faces, send, own, picked, sems):
    enter(0, live, slots, feat, field, faces, own, picked, sems)
    offer(jnp.where(picked[0, 0] == picked[0, 1], 0, 1), faces, send)


def second_entry_kernel(
    after, live, slots, feat, weights, neighbours, field, faces, held, names, scalars, own, picked, sems, nbr, named, far
):
    look = pltpu.make_async_copy(neighbours, nbr, far.at[1])
    fetch = pltpu.make_async_copy(weights, held, far.at[0])
    look.start()
    fetch.start()
    enter(1, live, slots, feat, field, faces, own, picked, sems)
    places = places_of(picked[0, 0], picked[0, 1])
    look.wait()
    t = nbr[...]
    new = t
    for k in range(BRICK):
        new = jnp.where(t == places[k], k, new)
    for k, axis in enumerate(("space", "slab")):
        place = lax.axis_index(axis)
        turn = jnp.where(place % 2 == 0, 2, 0)
        low = jnp.where(place == 0, 12, 4 + 4 * k + turn)
        high = jnp.where(place == lax.axis_size(axis) - 1, 12, 6 + 4 * k - turn)
        for e in range(2):
            new = jnp.where(t == 4 + 4 * k + e, jnp.minimum(low + e, 12), new)
            new = jnp.where(t == 6 + 4 * k + e, jnp.minimum(high + e, 12), new)
    named[:, 0:26] = new
    hand = pltpu.make_async_copy(named, names, far.at[2])
    hand.start()
    for k in range(BRICK):
        scalars[PLACE + k] = places[k]
    scalars[SECOND] = jnp.where(picked[0, 0] == picked[0, 1], 0, 1)
    scalars[LIVE] = live[0]
    fetch.wait()
    hand.wait()


def make_taps(index, plain, taps, wide):
    low = lower_half((32, 128))
    zero = jnp.zeros((32, 128), F32)
    for t in range(9):
        even = [plain[pl.ds((3 * t + d) * 128 + index, 32, stride=4), :] for d in range(3)]
        odd = [pltpu.roll(rows, 64, 1) for rows in even]

        def rows(held, d):
            return held[d] if 0 <= d <= 2 else zero

        for w, base in ((0, 192), (1, 0), (2, 64), (3, 128)):
            wide[t % 2, pl.ds(base, 32, stride=2), :] = jnp.where(low, rows(even, w), rows(odd, w - 1))
            wide[t % 2, pl.ds(base + 1, 32, stride=2), :] = jnp.where(low, rows(odd, w), rows(even, w - 1))
        full = wide[t % 2]
        high = full.astype(BF16)
        taps[t, :, 0:128] = high
        taps[t, :, 128:256] = (full - high.astype(F32)).astype(BF16)


def first_taps_kernel(weights, plain, taps, wide):
    for t in range(27):
        for i in range(32):
            plain[128 * t + 4 * i : 128 * t + 4 * i + 4, :] = weights[t, :, 128 * i : 128 * i + 128]
    make_taps(0, plain, taps, wide)


def taps_kernel(index, after, plain, taps, wide):
    make_taps(index, plain, taps, wide)


def fill_table(faces, arrived, table):
    for k, ref in enumerate(faces):
        table[2 * k : 2 * k + 2] = ref[...]
    for k, ref in zip(ORDER, arrived):
        for e in range(2):
            unpack(ref, e, table, 4 + 2 * k + e)
    table[12] = jnp.zeros((FACE, 128), F32)


def fill_margins(pair, names, scalars, field, table, one, two):
    for x in range(8):
        one[(x + 1) * 80 + 8 : (x + 1) * 80 + 72, :] = field[x * 64 : x * 64 + 64, :]
    for b in range(2):
        near = scalars[PLACE + 2 * pair + b]

        def cell(xp, yp):
            return (xp * 10 + yp) * 8 + 4 * b

        for d in (-1, 1):
            s, p = (1, 0) if d < 0 else (0, 9)
            t = names[near, direction(d, 0, 0)]
            for i in range(8):
                at = cell(p, i + 1)
                one[at : at + 4, :] = table[t, 32 * s + 4 * i : 32 * s + 4 * i + 4, :]
            t = names[near, direction(0, d, 0)]
            for i in range(8):
                at = cell(i + 1, p)
                one[at : at + 4, :] = table[t, 64 + 32 * s + 4 * i : 64 + 32 * s + 4 * i + 4, :]
            for e in (-1, 1):
                y, py = (7, 0) if e < 0 else (0, 9)
                t = names[near, direction(d, e, 0)]
                at = cell(p, py)
                one[at : at + 4, :] = table[t, 32 * s + 4 * y : 32 * s + 4 * y + 4, :]
    low3 = lower_half((10, 8, 128))
    for c in range(10):
        rows = one[c * 80 : c * 80 + 80, :].reshape(10, 8, 128)
        both = jnp.where(low3, pltpu.roll(rows, 7, 1), pltpu.roll(rows, 1, 1))
        two[c * 80 : c * 80 + 80, :] = both.reshape(80, 128)
    low = lower_half((8, 128))
    low1 = lower_half((1, 128))
    for b in range(2):
        near = scalars[PLACE + 2 * pair + b]
        for dz in (-1, 1):
            def merge(start, stride, new):
                at = pl.ds(start, 8, stride=stride)
                old = two[at, :]
                two[at, :] = jnp.where(low, new, old) if dz > 0 else jnp.where(low, old, new)

            row = 4 * b + (3 if dz > 0 else 0)
            t = names[near, direction(0, 0, dz)]
            for x in range(8):
                merge(((x + 1) * 10 + 1) * 8 + row, 8, table[t, 128 + 8 * x : 136 + 8 * x, :])
            for d in (-1, 1):
                x, p = (7, 0) if d < 0 else (0, 9)
                t = names[near, direction(d, 0, dz)]
                merge((p * 10 + 1) * 8 + row, 8, table[t, 128 + 8 * x : 136 + 8 * x, :])
                t = names[near, direction(0, d, dz)]
                merge((10 + p) * 8 + row, 80, table[t, pl.ds(128 + x, 8, stride=8), :])
                for e in (-1, 1):
                    y, py = (7, 0) if e < 0 else (0, 9)
                    t = names[near, direction(d, e, dz)]
                    at = (p * 10 + py) * 8 + row
                    new = table[t, 128 + 8 * x + y : 129 + 8 * x + y, :]
                    old = two[at : at + 1, :]
                    two[at : at + 1, :] = jnp.where(low1, new, old) if dz > 0 else jnp.where(low1, old, new)


def split(one, two, high, rest, mid_high, mid_rest):
    for c in range(10):
        for half, ref in enumerate((one, two)):
            lanes = slice(128 * half, 128 * half + 128)
            full = ref[c * 80 : c * 80 + 80, :]
            top = full.astype(BF16)
            high[c, :, lanes] = top
            rest[c, :, lanes] = (full - top.astype(F32)).astype(BF16)
            full = ref[c * 80 + 8 : c * 80 + 72, :]
            top = full.astype(BF16)
            mid_high[c, :, lanes] = top
            mid_rest[c, :, lanes] = (full - top.astype(F32)).astype(BF16)


def convolve(high, rest, mid_high, mid_rest, taps):
    def rows(ref, mid, dx, dy, planes=8):
        if dy == 1:
            return mid[dx : dx + planes].reshape(64 * planes, 256)
        return ref[dx : dx + planes, 8 * dy : 8 * dy + 64, :].reshape(64 * planes, 256)

    def product(left, right):
        return jnp.dot(left, right, preferred_element_type=F32)

    wide = None
    for dx in range(3):
        for dy in range(3):
            part = product(rows(high, mid_high, dx, dy), taps[3 * dx + dy])
            wide = part if wide is None else wide + part
    total = wide[:, 0:128] + wide[:, 128:256]
    for dy in range(3):
        two = jnp.concatenate([taps[dy, :, 0:128], taps[3 + dy, :, 0:128]], 1)
        part = product(rows(rest, mid_rest, 0, dy, 9), two)
        total = total + (part[0:512, 0:128] + part[64:576, 128:256])
    two = jnp.concatenate([taps[6, :, 0:128], taps[7, :, 0:128]], 1)
    part = product(rest[2:10].reshape(640, 256), two).reshape(8, 80, 256)
    total = total + (part[:, 0:64, 0:128] + part[:, 8:72, 128:256]).reshape(512, 128)
    return total + product(rows(rest, mid_rest, 2, 2), taps[8, :, 0:128])


def run_pair(pair, index, names, scalars, field, table, taps, biases, skip, new, work):
    one, two, high, rest, mid_high, mid_rest = work
    fill_margins(pair, names, scalars, field, table, one, two)
    split(one, two, high, rest, mid_high, mid_rest)
    total = convolve(high, rest, mid_high, mid_rest, taps)
    bias = biases[index : index + 1, :]
    total = total + jnp.concatenate([bias, bias], 1)
    if skip is not None:
        total = total + skip[...]
    second = lax.broadcasted_iota(jnp.int32, (512, 128), 0) % 8 >= 4
    slot = jnp.where(second, scalars[PLACE + 2 * pair + 1], scalars[PLACE + 2 * pair])
    new[...] = jnp.where(slot < scalars[LIVE], jnp.maximum(total, 0.0), 0.0)


def near_kernel(residual, index, names, scalars, field, faces_a, faces_b, *refs):
    arrived, (taps, biases), refs = refs[:4], refs[4:6], refs[6:]
    skip, refs = (refs[0], refs[1:]) if residual else (None, refs)
    new, faces, send, table = refs[:4]
    fill_table((faces_a, faces_b), arrived, table)
    run_pair(0, index, names, scalars, field, table, taps, biases, skip, new, refs[4:])
    write_faces(new, faces)
    offer(scalars[SECOND], faces, send)


def far_kernel(residual, index, names, scalars, field, table, taps, biases, *refs):
    skip, refs = (refs[0], refs[1:]) if residual else (None, refs)
    new, faces = refs[:2]
    run_pair(1, index, names, scalars, field, table, taps, biases, skip, new, refs[2:])
    write_faces(new, faces)


def last_kernel(index, names, scalars, field_a, field_b, faces_a, faces_b, *refs):
    arrived, (taps, biases, skip_a, skip_b, out, table, new_a, new_b, stage, sems), work = refs[:4], refs[4:14], refs[14:]
    fill_table((faces_a, faces_b), arrived, table)
    copies = []
    for pair, field, skip, new in ((0, field_a, skip_a, new_a), (1, field_b, skip_b, new_b)):
        own = work[6 * pair : 6 * pair + 6]
        run_pair(pair, index, names, scalars, field, table, taps, biases, skip, new, own)
        for b in range(2):
            at = 2 * pair + b
            for x in range(8):
                for q in range(4):
                    stage[at, x, :, 128 * q : 128 * q + 128] = new[pl.ds(x * 64 + 4 * b + q, 8, stride=8), :]
            copies.append(pltpu.make_async_copy(stage.at[at], out.at[scalars[PLACE + at]], sems.at[at]))
            copies[-1].start()
    for copy in copies:
        copy.wait()


FIELD = jax.ShapeDtypeStruct((512, 128), F32)
FACES = jax.ShapeDtypeStruct((2, FACE, 128), F32)
SEND = jax.ShapeDtypeStruct((2, PACK, 128), F32)
TABLE = jax.ShapeDtypeStruct((13, FACE, 128), F32)
WORK = [
    pltpu.VMEM((800, 128), F32),
    pltpu.VMEM((800, 128), F32),
    pltpu.VMEM((10, 80, 256), BF16),
    pltpu.VMEM((10, 80, 256), BF16),
    pltpu.VMEM((10, 64, 256), BF16),
    pltpu.VMEM((10, 64, 256), BF16),
]


def swaps(along, first):
    spaces, slabs = lax.axis_size("space"), lax.axis_size("slab")
    pairs = []
    for space in range(spaces):
        for slab in range(slabs):
            place, size = ((space, spaces), (slab, slabs))[along]
            other = place + 1 if (place - first) % 2 == 0 else place - 1
            if 0 <= other < size:
                to = ((other, slab), (space, other))[along]
            else:
                to = ((space, slab ^ 1), (space ^ 1, slab))[along]
            pairs.append((space * slabs + slab, to[0] * slabs + to[1]))
    return pairs


def exchange(send):
    got = [lax.ppermute(send, ("space", "slab"), swaps(at // 2, at % 2)) for at in range(4)]
    return [got[at] for at in ORDER]


def shards(features, live, rim_slots, neighbours, weights, biases):
    params = pltpu.CompilerParams(vmem_limit_bytes=24 * MIB)
    cost = pl.CostEstimate(flops=600_000_000, bytes_accessed=4 * MIB, transcendentals=0)
    convs = weights.shape[0]
    in_hbm = lambda array: pltpu.with_memory_space_constraint(array, pltpu.HBM)

    def call(kernel, name, out_shape, in_specs, scratch, args, out_specs=None):
        return pl.pallas_call(
            kernel,
            out_shape=out_shape,
            in_specs=in_specs,
            out_specs=tuple(VM for _ in out_shape) if out_specs is None else out_specs,
            scratch_shapes=scratch,
            compiler_params=params,
            cost_estimate=cost,
            name=name,
        )(*args)

    entry_scratch = [
        pltpu.VMEM(features.shape, F32),
        pltpu.SMEM((1, 2), jnp.int32),
        pltpu.SemaphoreType.DMA((2,)),
    ]
    field_a, faces_a, send = call(
        entry_kernel, "entry", (FIELD, FACES, SEND), [SM, HB, HB], entry_scratch,
        (live, in_hbm(rim_slots), in_hbm(features)),
    )
    turned = jnp.transpose(weights, (1, 0, 2))
    field_b, faces_b, held, names, scalars = call(
        second_entry_kernel,
        "second_entry",
        (FIELD, FACES, jax.ShapeDtypeStruct(turned.shape, F32), pltpu.SMEM((BRICK, 128), jnp.int32), pltpu.SMEM((LIVE + 1,), jnp.int32)),
        [pl.BlockSpec(memory_space=pl.ANY), SM, HB, HB, HB, HB],
        entry_scratch
        + [
            pltpu.VMEM(neighbours.shape, jnp.int32),
            pltpu.VMEM((BRICK, 128), jnp.int32),
            pltpu.SemaphoreType.DMA((3,)),
        ],
        (send, live, in_hbm(rim_slots), in_hbm(features), in_hbm(turned), in_hbm(neighbours)),
        (VM, VM, VM, SM, SM),
    )
    plain = None

    def taps_of(index, send):
        nonlocal plain
        shape = jax.ShapeDtypeStruct((9, 256, 256), BF16)
        scratch = [pltpu.VMEM((2, 256, 128), F32)]
        if index == 0:
            wide = jax.ShapeDtypeStruct((27 * 32 * convs, 128), F32)
            plain, taps = call(first_taps_kernel, "taps0", (wide, shape), [VM], scratch, (held,))
            return taps
        kernel = functools.partial(taps_kernel, index)
        specs = [pl.BlockSpec(memory_space=pl.ANY), VM]
        return call(kernel, f"taps{index}", (shape,), specs, scratch, (send, plain))[0]

    def layer(index, fields, faces, send, skips):
        arrived = exchange(send)
        taps = taps_of(index, send)
        args = [names, scalars, fields[0], *faces, *arrived, taps, biases]
        if skips is not None:
            args.append(skips[0])
        kernel = functools.partial(near_kernel, skips is not None, index)
        specs = [SM, SM] + [VM] * (len(args) - 2)
        new_a, faces_a, send, table = call(
            kernel, f"near{index}", (FIELD, FACES, SEND, TABLE), specs, WORK, args
        )
        args = [names, scalars, fields[1], table, taps, biases]
        if skips is not None:
            args.append(skips[1])
        kernel = functools.partial(far_kernel, skips is not None, index)
        specs = [SM, SM] + [VM] * (len(args) - 2)
        new_b, faces_b = call(kernel, f"far{index}", (FIELD, FACES), specs, WORK, args)
        return (new_a, new_b), (faces_a, faces_b), send

    def finish(index, fields, faces, send, skips):
        arrived = exchange(send)
        taps = taps_of(index, send)
        args = [names, scalars, *fields, *faces, *arrived, taps, biases, *skips]
        scratch = [
            pltpu.VMEM(TABLE.shape, F32),
            pltpu.VMEM(FIELD.shape, F32),
            pltpu.VMEM(FIELD.shape, F32),
            pltpu.VMEM(features.shape, F32),
            pltpu.SemaphoreType.DMA((BRICK,)),
        ]
        out = (jax.ShapeDtypeStruct(features.shape, F32),)
        kernel = functools.partial(last_kernel, index)
        specs = [SM, SM] + [VM] * (len(args) - 2)
        return call(kernel, f"last{index}", out, specs, scratch + WORK + WORK, args, (HB,))[0]

    state = (field_a, field_b), (faces_a, faces_b), send
    for index in range(0, convs, 2):
        skips = state[0]
        state = layer(index, *state, None)
        if index + 2 == convs:
            return finish(index + 1, *state, skips)
        state = layer(index + 1, *state, skips)


def solution(mesh):
    in_specs = (
        P(("space", "slab"), None, None, None),
        P(("space", "slab")),
        P(("space", "slab"), None),
        P(("space", "slab"), None),
        P(),
        P(),
    )
    out_specs = P(("space", "slab"), None, None, None)
    return jax.shard_map(shards, mesh=mesh, in_specs=in_specs, out_specs=out_specs, check_vma=False)
```

```python
import functools

import jax
import jax.numpy as jnp
from jax import lax
from jax.experimental import pallas as pl
from jax.experimental.pallas import tpu as pltpu
from jax.sharding import PartitionSpec as P

BRICK = 4
FACE = 192
PACK = 152
MIB = 1 << 20
VM = pl.BlockSpec(memory_space=pltpu.VMEM)
SM = pl.BlockSpec(memory_space=pltpu.SMEM)
HB = pl.BlockSpec(memory_space=pltpu.HBM)
F32, BF16 = jnp.float32, jnp.bfloat16
ORDER = [3, 0, 2, 1]
PLACE, SECOND, LIVE = 0, 4, 5


def direction(dx, dy, dz):
    at = (dx + 1) * 9 + (dy + 1) * 3 + dz + 1
    return at - (at > 13)


def lower_half(shape):
    return lax.broadcasted_iota(jnp.int32, shape, len(shape) - 1) < 64


def write_faces(field, faces):
    low = lower_half((8, 128))
    for b in range(2):
        for s in range(2):
            for i in range(8):
                col = (7 * s * 8 + i) * 8 + 4 * b
                faces[b, 32 * s + 4 * i : 32 * s + 4 * i + 4, :] = field[col : col + 4, :]
                col = (i * 8 + 7 * s) * 8 + 4 * b
                at = 64 + 32 * s + 4 * i
                faces[b, at : at + 4, :] = field[col : col + 4, :]
        for x in range(8):
            first = field[pl.ds(x * 64 + 4 * b, 8, stride=8), :]
            last = field[pl.ds(x * 64 + 4 * b + 3, 8, stride=8), :]
            faces[b, 128 + 8 * x : 136 + 8 * x, :] = jnp.where(low, first, last)


def offer(second, faces, send):
    for e, b in ((0, 0), (1, second)):
        send[e, 0:64, :] = faces[b, 0:64, :]
        for s in range(2):
            send[e, 64 + 24 * s : 88 + 24 * s, :] = faces[b, 68 + 32 * s : 92 + 32 * s, :]
        for x in range(6):
            at = 128 + 8 * (x + 1) + 1
            send[e, 112 + 6 * x : 118 + 6 * x, :] = faces[b, at : at + 6, :]
        send[e, 148:152, :] = jnp.zeros((4, 128), F32)


def unpack(pack, e, table, t):
    low = lower_half((8, 128))
    table[t, 0:64, :] = pack[e, 0:64, :]
    for s in range(2):
        table[t, 68 + 32 * s : 92 + 32 * s, :] = pack[e, 64 + 24 * s : 88 + 24 * s, :]
        for x in range(2):
            at = 64 + 32 * s + 28 * x
            table[t, at : at + 4, :] = pack[e, 32 * x + 28 * s : 32 * x + 28 * s + 4, :]
    for x in range(6):
        at = 128 + 8 * (x + 1) + 1
        table[t, at : at + 6, :] = pack[e, 112 + 6 * x : 118 + 6 * x, :]
    for s in range(2):
        first = table[t, pl.ds(64 + 32 * s, 8, stride=4), :]
        last = table[t, pl.ds(64 + 32 * s + 3, 8, stride=4), :]
        table[t, pl.ds(128 + 7 * s, 8, stride=8), :] = jnp.where(low, first, last)
        first = table[t, pl.ds(32 * s, 8, stride=4), :]
        last = table[t, pl.ds(32 * s + 3, 8, stride=4), :]
        table[t, 128 + 56 * s : 136 + 56 * s, :] = jnp.where(low, first, last)


def places_of(s0, s1):
    p0 = s0
    p1 = jnp.where(s1 == s0, (s0 + 1) % BRICK, s1)

    def free(slot):
        return (p0 != slot) & (p1 != slot)

    p2 = jnp.where(free(0), 0, jnp.where(free(1), 1, 2))
    return p0, p1, p2, 6 - p0 - p1 - p2


def enter(pair, live, slots, feat, field, faces, own, picked, sems):
    pick = pltpu.make_async_copy(slots, picked, sems.at[0])
    pick.start()
    copy = pltpu.make_async_copy(feat, own, sems.at[1])
    copy.start()
    pick.wait()
    places = places_of(picked[0, 0], picked[0, 1])
    copy.wait()
    for b in range(2):
        place = places[2 * pair + b]
        keep = jnp.where(place < live[0], 1.0, 0.0).astype(F32)
        for x in range(8):
            for q in range(4):
                tile = own[place, x, :, 128 * q : 128 * q + 128] * keep
                field[pl.ds(x * 64 + 4 * b + q, 8, stride=8), :] = tile
    write_faces(field, faces)


def entry_kernel(live, slots, feat, field, faces, send, own, picked, sems):
    enter(0, live, slots, feat, field, faces, own, picked, sems)
    offer(jnp.where(picked[0, 0] == picked[0, 1], 0, 1), faces, send)


def second_entry_kernel(
    after, live, slots, feat, weights, neighbours, field, faces, held, names, scalars, own, picked, sems, nbr, named, far
):
    look = pltpu.make_async_copy(neighbours, nbr, far.at[1])
    fetch = pltpu.make_async_copy(weights, held, far.at[0])
    look.start()
    fetch.start()
    enter(1, live, slots, feat, field, faces, own, picked, sems)
    places = places_of(picked[0, 0], picked[0, 1])
    look.wait()
    t = nbr[...]
    new = t
    for k in range(BRICK):
        new = jnp.where(t == places[k], k, new)
    for k, axis in enumerate(("space", "slab")):
        place = lax.axis_index(axis)
        turn = jnp.where(place % 2 == 0, 2, 0)
        low = jnp.where(place == 0, 12, 4 + 4 * k + turn)
        high = jnp.where(place == lax.axis_size(axis) - 1, 12, 6 + 4 * k - turn)
        for e in range(2):
            new = jnp.where(t == 4 + 4 * k + e, jnp.minimum(low + e, 12), new)
            new = jnp.where(t == 6 + 4 * k + e, jnp.minimum(high + e, 12), new)
    named[:, 0:26] = new
    hand = pltpu.make_async_copy(named, names, far.at[2])
    hand.start()
    for k in range(BRICK):
        scalars[PLACE + k] = places[k]
    scalars[SECOND] = jnp.where(picked[0, 0] == picked[0, 1], 0, 1)
    scalars[LIVE] = live[0]
    fetch.wait()
    hand.wait()


def make_taps(index, plain, taps, wide):
    low = lower_half((32, 128))
    zero = jnp.zeros((32, 128), F32)
    for t in range(9):
        even = [plain[pl.ds((3 * t + d) * 128 + index, 32, stride=4), :] for d in range(3)]
        odd = [pltpu.roll(rows, 64, 1) for rows in even]

        def rows(held, d):
            return held[d] if 0 <= d <= 2 else zero

        for w, base in ((0, 192), (1, 0), (2, 64), (3, 128)):
            wide[t % 2, pl.ds(base, 32, stride=2), :] = jnp.where(low, rows(even, w), rows(odd, w - 1))
            wide[t % 2, pl.ds(base + 1, 32, stride=2), :] = jnp.where(low, rows(odd, w), rows(even, w - 1))
        full = wide[t % 2]
        high = full.astype(BF16)
        taps[t, :, 0:128] = high
        taps[t, :, 128:256] = (full - high.astype(F32)).astype(BF16)


def first_taps_kernel(weights, plain, taps, wide):
    for t in range(27):
        for i in range(32):
            plain[128 * t + 4 * i : 128 * t + 4 * i + 4, :] = weights[t, :, 128 * i : 128 * i + 128]
    make_taps(0, plain, taps, wide)


def taps_kernel(index, after, plain, taps, wide):
    make_taps(index, plain, taps, wide)


def fill_table(faces, arrived, table):
    for k, ref in enumerate(faces):
        table[2 * k : 2 * k + 2] = ref[...]
    for k, ref in zip(ORDER, arrived):
        for e in range(2):
            unpack(ref, e, table, 4 + 2 * k + e)
    table[12] = jnp.zeros((FACE, 128), F32)


def fill_margins(pair, names, scalars, field, table, one, two):
    for x in range(8):
        one[(x + 1) * 80 + 8 : (x + 1) * 80 + 72, :] = field[x * 64 : x * 64 + 64, :]
    for b in range(2):
        near = scalars[PLACE + 2 * pair + b]

        def cell(xp, yp):
            return (xp * 10 + yp) * 8 + 4 * b

        for d in (-1, 1):
            s, p = (1, 0) if d < 0 else (0, 9)
            t = names[near, direction(d, 0, 0)]
            for i in range(8):
                at = cell(p, i + 1)
                one[at : at + 4, :] = table[t, 32 * s + 4 * i : 32 * s + 4 * i + 4, :]
            t = names[near, direction(0, d, 0)]
            for i in range(8):
                at = cell(i + 1, p)
                one[at : at + 4, :] = table[t, 64 + 32 * s + 4 * i : 64 + 32 * s + 4 * i + 4, :]
            for e in (-1, 1):
                y, py = (7, 0) if e < 0 else (0, 9)
                t = names[near, direction(d, e, 0)]
                at = cell(p, py)
                one[at : at + 4, :] = table[t, 32 * s + 4 * y : 32 * s + 4 * y + 4, :]
    low3 = lower_half((10, 8, 128))
    for c in range(10):
        rows = one[c * 80 : c * 80 + 80, :].reshape(10, 8, 128)
        both = jnp.where(low3, pltpu.roll(rows, 7, 1), pltpu.roll(rows, 1, 1))
        two[c * 80 : c * 80 + 80, :] = both.reshape(80, 128)
    low = lower_half((8, 128))
    low1 = lower_half((1, 128))
    for b in range(2):
        near = scalars[PLACE + 2 * pair + b]
        for dz in (-1, 1):
            def merge(start, stride, new):
                at = pl.ds(start, 8, stride=stride)
                old = two[at, :]
                two[at, :] = jnp.where(low, new, old) if dz > 0 else jnp.where(low, old, new)

            row = 4 * b + (3 if dz > 0 else 0)
            t = names[near, direction(0, 0, dz)]
            for x in range(8):
                merge(((x + 1) * 10 + 1) * 8 + row, 8, table[t, 128 + 8 * x : 136 + 8 * x, :])
            for d in (-1, 1):
                x, p = (7, 0) if d < 0 else (0, 9)
                t = names[near, direction(d, 0, dz)]
                merge((p * 10 + 1) * 8 + row, 8, table[t, 128 + 8 * x : 136 + 8 * x, :])
                t = names[near, direction(0, d, dz)]
                merge((10 + p) * 8 + row, 80, table[t, pl.ds(128 + x, 8, stride=8), :])
                for e in (-1, 1):
                    y, py = (7, 0) if e < 0 else (0, 9)
                    t = names[near, direction(d, e, dz)]
                    at = (p * 10 + py) * 8 + row
                    new = table[t, 128 + 8 * x + y : 129 + 8 * x + y, :]
                    old = two[at : at + 1, :]
                    two[at : at + 1, :] = jnp.where(low1, new, old) if dz > 0 else jnp.where(low1, old, new)


def split(one, two, high, rest, mid_high, mid_rest):
    for c in range(10):
        for half, ref in enumerate((one, two)):
            lanes = slice(128 * half, 128 * half + 128)
            full = ref[c * 80 : c * 80 + 80, :]
            top = full.astype(BF16)
            high[c, :, lanes] = top
            rest[c, :, lanes] = (full - top.astype(F32)).astype(BF16)
            full = ref[c * 80 + 8 : c * 80 + 72, :]
            top = full.astype(BF16)
            mid_high[c, :, lanes] = top
            mid_rest[c, :, lanes] = (full - top.astype(F32)).astype(BF16)


def convolve(high, rest, mid_high, mid_rest, taps):
    def rows(ref, mid, dx, dy, planes=8):
        if dy == 1:
            return mid[dx : dx + planes].reshape(64 * planes, 256)
        return ref[dx : dx + planes, 8 * dy : 8 * dy + 64, :].reshape(64 * planes, 256)

    def product(left, right):
        return jnp.dot(left, right, preferred_element_type=F32)

    wide = None
    for dx in range(3):
        for dy in range(3):
            part = product(rows(high, mid_high, dx, dy), taps[3 * dx + dy])
            wide = part if wide is None else wide + part
    total = wide[:, 0:128] + wide[:, 128:256]
    for dy in range(3):
        two = jnp.concatenate([taps[dy, :, 0:128], taps[3 + dy, :, 0:128]], 1)
        part = product(rows(rest, mid_rest, 0, dy, 9), two)
        total = total + (part[0:512, 0:128] + part[64:576, 128:256])
    two = jnp.concatenate([taps[6, :, 0:128], taps[7, :, 0:128]], 1)
    part = product(rest[2:10].reshape(640, 256), two).reshape(8, 80, 256)
    total = total + (part[:, 0:64, 0:128] + part[:, 8:72, 128:256]).reshape(512, 128)
    return total + product(rows(rest, mid_rest, 2, 2), taps[8, :, 0:128])


def run_pair(pair, index, names, scalars, field, table, taps, biases, skip, new, work):
    one, two, high, rest, mid_high, mid_rest = work
    fill_margins(pair, names, scalars, field, table, one, two)
    split(one, two, high, rest, mid_high, mid_rest)
    total = convolve(high, rest, mid_high, mid_rest, taps)
    bias = biases[index : index + 1, :]
    total = total + jnp.concatenate([bias, bias], 1)
    if skip is not None:
        total = total + skip[...]
    second = lax.broadcasted_iota(jnp.int32, (512, 128), 0) % 8 >= 4
    slot = jnp.where(second, scalars[PLACE + 2 * pair + 1], scalars[PLACE + 2 * pair])
    new[...] = jnp.where(slot < scalars[LIVE], jnp.maximum(total, 0.0), 0.0)


def near_kernel(residual, index, names, scalars, field, faces_a, faces_b, *refs):
    arrived, (taps, biases), refs = refs[:4], refs[4:6], refs[6:]
    skip, refs = (refs[0], refs[1:]) if residual else (None, refs)
    new, faces, send, table = refs[:4]
    fill_table((faces_a, faces_b), arrived, table)
    run_pair(0, index, names, scalars, field, table, taps, biases, skip, new, refs[4:])
    write_faces(new, faces)
    offer(scalars[SECOND], faces, send)


def far_kernel(residual, index, names, scalars, field, table, taps, biases, *refs):
    skip, refs = (refs[0], refs[1:]) if residual else (None, refs)
    new, faces = refs[:2]
    run_pair(1, index, names, scalars, field, table, taps, biases, skip, new, refs[2:])
    write_faces(new, faces)


def last_kernel(index, names, scalars, field_a, field_b, faces_a, faces_b, *refs):
    arrived, (taps, biases, skip_a, skip_b, out, table, new_a, new_b, stage, sems), work = refs[:4], refs[4:14], refs[14:]
    fill_table((faces_a, faces_b), arrived, table)
    copies = []
    for pair, field, skip, new in ((0, field_a, skip_a, new_a), (1, field_b, skip_b, new_b)):
        own = work[6 * pair : 6 * pair + 6]
        run_pair(pair, index, names, scalars, field, table, taps, biases, skip, new, own)
        for b in range(2):
            at = 2 * pair + b
            for x in range(8):
                for q in range(4):
                    stage[at, x, :, 128 * q : 128 * q + 128] = new[pl.ds(x * 64 + 4 * b + q, 8, stride=8), :]
            copies.append(pltpu.make_async_copy(stage.at[at], out.at[scalars[PLACE + at]], sems.at[at]))
            copies[-1].start()
    for copy in copies:
        copy.wait()


FIELD = jax.ShapeDtypeStruct((512, 128), F32)
FACES = jax.ShapeDtypeStruct((2, FACE, 128), F32)
SEND = jax.ShapeDtypeStruct((2, PACK, 128), F32)
TABLE = jax.ShapeDtypeStruct((13, FACE, 128), F32)
WORK = [
    pltpu.VMEM((800, 128), F32),
    pltpu.VMEM((800, 128), F32),
    pltpu.VMEM((10, 80, 256), BF16),
    pltpu.VMEM((10, 80, 256), BF16),
    pltpu.VMEM((10, 64, 256), BF16),
    pltpu.VMEM((10, 64, 256), BF16),
]


def swaps(along, first):
    spaces, slabs = lax.axis_size("space"), lax.axis_size("slab")
    pairs = []
    for space in range(spaces):
        for slab in range(slabs):
            place, size = ((space, spaces), (slab, slabs))[along]
            other = place + 1 if (place - first) % 2 == 0 else place - 1
            if 0 <= other < size:
                to = ((other, slab), (space, other))[along]
            else:
                to = ((space, slab ^ 1), (space ^ 1, slab))[along]
            pairs.append((space * slabs + slab, to[0] * slabs + to[1]))
    return pairs


def exchange(send):
    got = [lax.ppermute(send, ("space", "slab"), swaps(at // 2, at % 2)) for at in range(4)]
    return [got[at] for at in ORDER]


def shards(features, live, rim_slots, neighbours, weights, biases):
    params = pltpu.CompilerParams(vmem_limit_bytes=24 * MIB)
    cost = pl.CostEstimate(flops=600_000_000, bytes_accessed=4 * MIB, transcendentals=0)
    convs = weights.shape[0]
    in_hbm = lambda array: pltpu.with_memory_space_constraint(array, pltpu.HBM)

    def call(kernel, name, out_shape, in_specs, scratch, args, out_specs=None):
        return pl.pallas_call(
            kernel,
            out_shape=out_shape,
            in_specs=in_specs,
            out_specs=tuple(VM for _ in out_shape) if out_specs is None else out_specs,
            scratch_shapes=scratch,
            compiler_params=params,
            cost_estimate=cost,
            name=name,
        )(*args)

    entry_scratch = [
        pltpu.VMEM(features.shape, F32),
        pltpu.SMEM((1, 2), jnp.int32),
        pltpu.SemaphoreType.DMA((2,)),
    ]
    field_a, faces_a, send = call(
        entry_kernel, "entry", (FIELD, FACES, SEND), [SM, HB, HB], entry_scratch,
        (live, in_hbm(rim_slots), in_hbm(features)),
    )
    turned = jnp.transpose(weights, (1, 0, 2))
    field_b, faces_b, held, names, scalars = call(
        second_entry_kernel,
        "second_entry",
        (FIELD, FACES, jax.ShapeDtypeStruct(turned.shape, F32), pltpu.SMEM((BRICK, 128), jnp.int32), pltpu.SMEM((LIVE + 1,), jnp.int32)),
        [pl.BlockSpec(memory_space=pl.ANY), SM, HB, HB, HB, HB],
        entry_scratch
        + [
            pltpu.VMEM(neighbours.shape, jnp.int32),
            pltpu.VMEM((BRICK, 128), jnp.int32),
            pltpu.SemaphoreType.DMA((3,)),
        ],
        (send, live, in_hbm(rim_slots), in_hbm(features), in_hbm(turned), in_hbm(neighbours)),
        (VM, VM, VM, SM, SM),
    )
    plain = None

    def taps_of(index, send):
        nonlocal plain
        shape = jax.ShapeDtypeStruct((9, 256, 256), BF16)
        scratch = [pltpu.VMEM((2, 256, 128), F32)]
        if index == 0:
            wide = jax.ShapeDtypeStruct((27 * 32 * convs, 128), F32)
            plain, taps = call(first_taps_kernel, "taps0", (wide, shape), [VM], scratch, (held,))
            return taps
        kernel = functools.partial(taps_kernel, index)
        specs = [pl.BlockSpec(memory_space=pl.ANY), VM]
        return call(kernel, f"taps{index}", (shape,), specs, scratch, (send, plain))[0]

    def layer(index, fields, faces, send, skips):
        arrived = exchange(send)
        taps = taps_of(index, send)
        args = [names, scalars, fields[0], *faces, *arrived, taps, biases]
        if skips is not None:
            args.append(skips[0])
        kernel = functools.partial(near_kernel, skips is not None, index)
        specs = [SM, SM] + [VM] * (len(args) - 2)
        new_a, faces_a, send, table = call(
            kernel, f"near{index}", (FIELD, FACES, SEND, TABLE), specs, WORK, args
        )
        args = [names, scalars, fields[1], table, taps, biases]
        if skips is not None:
            args.append(skips[1])
        kernel = functools.partial(far_kernel, skips is not None, index)
        specs = [SM, SM] + [VM] * (len(args) - 2)
        new_b, faces_b = call(kernel, f"far{index}", (FIELD, FACES), specs, WORK, args)
        return (new_a, new_b), (faces_a, faces_b), send

    def finish(index, fields, faces, send, skips):
        arrived = exchange(send)
        taps = taps_of(index, send)
        args = [names, scalars, *fields, *faces, *arrived, taps, biases, *skips]
        scratch = [
            pltpu.VMEM(TABLE.shape, F32),
            pltpu.VMEM(FIELD.shape, F32),
            pltpu.VMEM(FIELD.shape, F32),
            pltpu.VMEM(features.shape, F32),
            pltpu.SemaphoreType.DMA((BRICK,)),
        ]
        out = (jax.ShapeDtypeStruct(features.shape, F32),)
        kernel = functools.partial(last_kernel, index)
        specs = [SM, SM] + [VM] * (len(args) - 2)
        return call(kernel, f"last{index}", out, specs, scratch + WORK + WORK, args, (HB,))[0]

    state = (field_a, field_b), (faces_a, faces_b), send
    for index in range(0, convs, 2):
        skips = state[0]
        state = layer(index, *state, None)
        if index + 2 == convs:
            return finish(index + 1, *state, skips)
        state = layer(index + 1, *state, skips)


def solution(mesh):
    in_specs = (
        P(("space", "slab"), None, None, None),
        P(("space", "slab")),
        P(("space", "slab"), None),
        P(("space", "slab"), None),
        P(),
        P(),
    )
    out_specs = P(("space", "slab"), None, None, None)
    return jax.shard_map(shards, mesh=mesh, in_specs=in_specs, out_specs=out_specs, check_vma=False)
```
